256 devices in a mesh: dp: 8 (over z_lo, x), ctx: 32 (over y, z_hi, core).
Axes of the slice: x: 4, y: 4, z: 8 (z_hi: 4, z_lo: 2; z = z_hi * 2 + z_lo), core: 2. Of those that a mesh axis runs over, the one named last changes fastest.
Arguments:
- vit_states: bfloat16 [8, 4096, 2560], P('dp', 'ctx')
- norm_gain: float32 [640], replicated, may hold values from 0.5 to 1.5
- w_first: bfloat16 [2560, 2560], P('dp'), may hold values from -0.125 to 0.125
- b_first: float32 [2560], P('dp'), may hold values from -3 to 3
- w_second: bfloat16 [2560, 4096], P('dp'), may hold values from -0.125 to 0.125
- llm_grad: bfloat16 [8, 4096, 4096], P('dp', 'ctx'), may hold values from -6 to 6
- block_order: int32 [64], replicated, may hold values from 0 to 63, as said below
- frame_tokens: int32 [8, 128], replicated, may hold values from 8 to 32, as said below
Outputs:
- vit_grad: bfloat16 [8, 4096, 2560], P('dp', 'ctx')
- w_first_grad: float32 [2560, 2560], P('dp', 'ctx')
- w_second_grad: float32 [2560, 4096], P('dp', 'ctx')
The draws below stay inside these ranges and needn't reach their ends.
Inputs may be any that keep to these rules, and one draw needn't show every extreme that they name: `block_order`: a permutation of 0 to 63 in which entries 2 c and 2 c + 1 add up to 63 for every c. `frame_tokens`: every video has a frame with all 32 slots used.
All inputs are finite; a program needn't handle non-finite values.
Results may differ from the reference program's by a relative error of at most 0.02.
Values may be sent and summed in bfloat16 or wider, within the bound.
A program may use at most 128 MiB of HBM per device.

```python
import math
import jax
import jax.numpy as jnp
from jax import lax

D_VIT = 640
HID = 2560
D_LLM = 4096
FRAME_SLOTS = 32
MERGE_IN = 2560
GROUPS = 8
VIDEOS = 8
MERGED = 4096
BLOCKS = 64
BLOCK_ROWS = 64
FRAMES = 128


def draw_vit_states(key, part):
    key = jax.random.fold_in(key, 3)
    base_key, row_key, col_key = jax.random.split(key, 3)
    base_values = jax.random.normal(base_key, (VIDEOS, MERGED, 4, D_VIT), jnp.float32)
    upper_log = math.log(10.0)
    row_scale = jnp.exp(jax.random.uniform(row_key, (VIDEOS, MERGED, 4, 1), jnp.float32, 0.0, upper_log))
    col_scale = jnp.exp(jax.random.uniform(col_key, (1, 1, 1, D_VIT), jnp.float32, 0.0, math.log(4.0)))
    return (base_values * row_scale * col_scale).reshape(VIDEOS, MERGED, MERGE_IN).astype(jnp.bfloat16)


def draw_block_order(key, part):
    key = jax.random.fold_in(key, 1)
    shuffled = jax.random.permutation(key, BLOCKS // 2).astype(jnp.int32)
    mirrored = BLOCKS - 1 - shuffled
    return jnp.stack([shuffled, mirrored], axis=1).reshape(BLOCKS).astype(jnp.int32)


def draw_frame_tokens(key, part):
    key = jax.random.fold_in(key, 2)
    count_key, full_key = jax.random.split(key, 2)
    counts = jax.random.randint(count_key, (VIDEOS, FRAMES), FRAME_SLOTS // 4, FRAME_SLOTS + 1, dtype=jnp.int32)
    full_frame = jax.random.randint(full_key, (VIDEOS,), 0, FRAMES, dtype=jnp.int32)
    frame_ids = jnp.arange(FRAMES, dtype=jnp.int32)
    return jnp.where(frame_ids[None, :] == full_frame[:, None], FRAME_SLOTS, counts).astype(jnp.int32)


def steps_of(stream_key, extent, cuts, least, largest):
    def one(dim, blocks):
        steps = jax.random.uniform(jax.random.fold_in(jax.random.fold_in(stream_key, 6), dim), (blocks,), jnp.float32, least / len(cuts), largest / len(cuts))
        return jnp.repeat(jnp.exp(steps), extent[dim] // blocks).reshape((-1,) + (1,) * (len(extent) - dim - 1))

    loudness = one(*cuts[0])
    for cut in cuts[1:]:
        loudness = loudness * one(*cut)
    return loudness


def bell_draw(rng, shape, width, limit, pieces=(), held_as=jnp.bfloat16):
    level = steps_of(rng, shape, pieces, -0.22, 0.18) if pieces else 1.0
    drawn = jax.random.normal(rng, shape, jnp.float32) * width * level
    return jnp.minimum(jnp.maximum(drawn, -limit), limit).astype(held_as)


def setup_inputs(seed: int = 0) -> dict:
    keys = jax.random.split(jax.random.key(seed), 9)
    vit_states = draw_vit_states(jax.random.fold_in(keys[8], 71), 0)
    norm_gain = jnp.clip(1.0 + 0.1 * jax.random.normal(keys[1], (D_VIT,), jnp.float32), 0.5, 1.5)
    w_first = bell_draw(keys[2], (HID, MERGE_IN), MERGE_IN ** -0.5, 0.125, ((0, 8),))
    b_first = bell_draw(keys[3], (HID,), 0.5, 3.0, ((0, 8),), jnp.float32)
    w_second = bell_draw(keys[4], (HID, D_LLM), HID ** -0.5, 0.125, ((0, 8),))
    llm_grad = bell_draw(keys[5], (VIDEOS, MERGED, D_LLM), 1.0, 6.0, ((0, 8), (1, 32)))
    block_order = draw_block_order(jax.random.fold_in(keys[8], 71), 0)
    frame_tokens = draw_frame_tokens(jax.random.fold_in(keys[8], 71), 0)
    return dict(vit_states=vit_states, norm_gain=norm_gain, w_first=w_first, b_first=b_first, w_second=w_second, llm_grad=llm_grad, block_order=block_order, frame_tokens=frame_tokens)


epsilon = 1e-06

def gelu_value(values):
    return 0.5 * values * (1.0 + jax.scipy.special.erf(values * (1.0 / math.sqrt(2.0))))

def gelu_slope(values):
    normal_cdf = 0.5 * (1.0 + jax.scipy.special.erf(values * (1.0 / math.sqrt(2.0))))
    density = jnp.exp(-0.5 * values * values) * (1.0 / math.sqrt(2.0 * math.pi))
    return normal_cdf + values * density

def grouped_product(pre_grad, w_first):
    group_width = HID // GROUPS

    def add_group(running, group_index):
        first_col = group_index * group_width
        grad_slab = lax.dynamic_slice_in_dim(pre_grad, first_col, group_width, 1)
        weight_rows = lax.dynamic_slice_in_dim(w_first, first_col, group_width, 0)
        partial_sum = jnp.dot(grad_slab, weight_rows, preferred_element_type=jnp.float32)
        rounded = lax.optimization_barrier(partial_sum.astype(jnp.bfloat16)).astype(jnp.float32)
        return (running + rounded, None)
    start_value = jnp.zeros((MERGED, MERGE_IN), jnp.float32)
    result, unused = lax.scan(add_group, start_value, jnp.arange(GROUPS, dtype=jnp.int32))
    return result

def reference(vit_states, norm_gain, w_first, b_first, w_second, llm_grad, block_order, frame_tokens):
    positions = jnp.arange(BLOCKS, dtype=jnp.int32)
    inverse = jnp.zeros((BLOCKS,), jnp.int32).at[block_order.astype(jnp.int32)].set(positions)
    slot_ids = jnp.arange(FRAME_SLOTS, dtype=jnp.int32)
    first_total = jnp.zeros((HID, MERGE_IN), jnp.float32)
    second_total = jnp.zeros((HID, D_LLM), jnp.float32)
    outputs = []
    for video_index in range(VIDEOS):
        llm_blocks = llm_grad[video_index].reshape(BLOCKS, BLOCK_ROWS, D_LLM)
        time_grad = jnp.take(llm_blocks, inverse, axis=0).reshape(MERGED, D_LLM)
        keep_rows = (slot_ids[None, :] < frame_tokens[video_index][:, None]).reshape(MERGED)
        masked = jnp.where(keep_rows[:, None], time_grad, jnp.zeros_like(time_grad))
        states = vit_states[video_index].astype(jnp.float32).reshape(MERGED, 4, D_VIT)
        inv_rms = lax.rsqrt(lax.optimization_barrier(jnp.mean(states * states, axis=-1, keepdims=True)) + epsilon)
        scaled = states * inv_rms
        normed = (scaled * norm_gain).astype(jnp.bfloat16).reshape(MERGED, MERGE_IN)
        pre_act = jnp.dot(normed, w_first.T, preferred_element_type=jnp.float32) + b_first
        activated = gelu_value(pre_act).astype(jnp.bfloat16)
        hidden_grad = jnp.dot(masked, w_second.T, preferred_element_type=jnp.float32)
        pre_grad = (hidden_grad * gelu_slope(pre_act)).astype(jnp.bfloat16)
        second_total = second_total + jnp.dot(activated.T, masked, preferred_element_type=jnp.float32)
        first_total = first_total + jnp.dot(pre_grad.T, normed, preferred_element_type=jnp.float32)
        normed_grad = grouped_product(pre_grad, w_first)
        scaled_grad = normed_grad.reshape(MERGED, 4, D_VIT) * norm_gain
        vit_rows = inv_rms * (scaled_grad - scaled * lax.optimization_barrier(jnp.mean(scaled_grad * scaled, axis=-1, keepdims=True)))
        outputs.append(vit_rows.astype(jnp.bfloat16).reshape(MERGED, MERGE_IN))
    return (jnp.stack(outputs), first_total, second_total)
```

```python
import functools
import math

import jax
import jax.numpy as jnp
from jax import lax
from jax.experimental import pallas as pl
from jax.experimental.pallas import tpu as pltpu
from jax.sharding import PartitionSpec as P

MESH = pl.DeviceIdType.MESH
EPS = 1e-06
X, Y, Z, CTX = 4, 4, 8, 32
ROWS = 128
SEG = 640
F32, BF16 = jnp.float32, jnp.bfloat16


def gelu_value(values):
    return 0.5 * values * (1.0 + lax.erf(values * (1.0 / math.sqrt(2.0))))


def gelu_slope(values):
    normal_cdf = 0.5 * (1.0 + lax.erf(values * (1.0 / math.sqrt(2.0))))
    density = jnp.exp(-0.5 * values * values) * (1.0 / math.sqrt(2.0 * math.pi))
    return normal_cdf + values * density


def place():
    dp, ctx = lax.axis_index("dp"), lax.axis_index("ctx")
    x, y, core = lax.rem(dp, X), ctx // 8, lax.rem(ctx, 2)
    z = lax.rem(ctx // 2, 4) * 2 + dp // X
    return x, y, z, core


def device(x, y, z, core):
    return (lax.rem(z, 2) * X + x, y * 8 + (z // 2) * 2 + core)


def greet(others):
    barrier = pltpu.get_barrier_semaphore()
    for other in others:
        pl.semaphore_signal(barrier, inc=1, device_id=other, device_id_type=MESH)
    return barrier


def remote(src, dst, send, recv, to):
    return pltpu.make_async_remote_copy(
        src_ref=src, dst_ref=dst, send_sem=send, recv_sem=recv, device_id=to, device_id_type=MESH
    )


def loop(n, body):
    lax.fori_loop(0, n, lambda i, c: (body(i), c)[1], 0)


def gather_kernel(
    inv, order, frames, llm, vit, gain, bias, w1, w2,
    llm_rows, n_rows, w1_all, w2_all, b_all,
    masked, normed, recv1, send2,
    s1, r1, s2, r2, loc, wsend, wrecv, nsend, nrecv, lsend, lrecv,
):
    x, y, z, core = place()
    ctx, dp = lax.axis_index("ctx"), lax.axis_index("dp")
    right, left = lax.rem(x + 1, X), lax.rem(x + X - 1, X)
    to_right, to_left = device(right, y, z, core), device(left, y, z, core)
    up, down = lax.rem(z + 1, Z), lax.rem(z + Z - 1, Z)
    z_to = jnp.where(core == 0, up, down)
    z_from = jnp.where(core == 0, down, up)
    to_z, from_z = device(x, y, z_to, core), device(x, y, z_from, core)
    sibling = device(x, y, z, 1 - core)

    barrier = greet([to_right, to_left, to_z, from_z])

    def hello(k):
        pl.semaphore_signal(
            barrier, inc=1, device_id=(dp, lax.rem(ctx + k + 1, CTX)), device_id_type=MESH
        )

    loop(CTX - 1, hello)

    for block in range(2):
        t = order[2 * ctx + block]
        for frame in range(2):
            count = frames[dp, 2 * t + frame]
            keep = lax.broadcasted_iota(jnp.int32, (32, 512), 0) < count

            def mask(c):
                at = (block, pl.ds(32 * frame, 32), pl.ds(pl.multiple_of(c * 512, 512), 512))
                masked[at] = jnp.where(keep, llm[at].astype(F32), 0.0).astype(BF16)

            loop(8, mask)

    pl.semaphore_wait(barrier, CTX - 1 + 4)

    def cols(i):
        return pl.ds(pl.multiple_of(i * 128, 128), 128)

    def first(k):
        t = lax.rem(ctx + k + 1, CTX)
        return remote(masked.at[:, :, cols(t)], recv1.at[ctx], s1.at[k], r1.at[ctx], (dp, t))

    loop(CTX - 1, lambda k: first(k).start())
    own1 = pltpu.make_async_copy(masked.at[:, :, cols(ctx)], recv1.at[ctx], loc.at[0])
    own1.start()

    def norm(i):
        rows = pl.ds(pl.multiple_of(i * 32, 32), 32)
        for seg in range(4):
            at = (rows, slice(seg * SEG, (seg + 1) * SEG))
            states = vit[at].astype(F32)
            inv_rms = lax.rsqrt(jnp.mean(states * states, axis=-1, keepdims=True) + EPS)
            normed[i // 2, pl.ds(pl.multiple_of(lax.rem(i, 2) * 32, 32), 32), at[1]] = (
                states * inv_rms * gain[...]
            ).astype(BF16)

    loop(4, norm)

    def spread(rows, own, send, recv, which):
        here = pltpu.make_async_copy(own, rows.at[x], loc.at[which])
        a = remote(own, rows.at[x], send.at[0], recv.at[0], to_right)
        b = remote(own, rows.at[x], send.at[1], recv.at[1], to_left)
        return here, a, b

    def forward(rows, send, recv):
        c = remote(rows.at[left, 0], rows.at[left, 0], send.at[2], recv.at[2], to_right)
        d = remote(rows.at[right, 1], rows.at[right, 1], send.at[3], recv.at[3], to_left)
        return c, d

    n_here, n_a, n_b = spread(n_rows, normed, nsend, nrecv, 1)
    for c in (n_here, n_a, n_b):
        c.start()

    keep_w = [
        pltpu.make_async_copy(src, dst.at[0], loc.at[2 + i])
        for i, (src, dst) in enumerate(((w1, w1_all), (w2, w2_all), (bias, b_all)))
    ]
    for c in keep_w:
        c.start()

    def first_here(k):
        s = lax.rem(ctx + k + 1, CTX)
        remote(masked.at[:, :, cols(0)], recv1.at[s], s1.at[k], r1.at[s], (dp, s)).wait_recv()

    loop(CTX - 1, first_here)
    own1.wait()

    def pick(d):
        for i in range(2):
            b = inv[2 * d + i]
            send2[d, i] = recv1[b // 2, lax.rem(b, 2)]

    def second(k):
        d = lax.rem(ctx + k + 1, CTX)
        return remote(
            send2.at[d], llm_rows.at[x, :, :, cols(ctx)], s2.at[k], r2.at[ctx], (dp, d)
        )

    def send_second(k):
        pick(lax.rem(ctx + k + 1, CTX))
        second(k).start()

    loop(CTX - 1, send_second)
    pick(ctx)
    own2 = pltpu.make_async_copy(send2.at[ctx], llm_rows.at[x, :, :, cols(ctx)], loc.at[5])
    own2.start()

    mine = pl.ds(pl.multiple_of(core * 160, 32), 160)
    theirs = pl.ds(pl.multiple_of((1 - core) * 160, 32), 160)
    w_copies = [
        remote(w1.at[mine], w1_all.at[1, mine], wsend.at[0], wrecv.at[0], to_z),
        remote(w2.at[mine], w2_all.at[1, mine], wsend.at[1], wrecv.at[1], to_z),
        remote(bias, b_all.at[1], wsend.at[2], wrecv.at[2], to_z),
    ]
    for c in w_copies:
        c.start()

    n_a.wait_recv()
    n_b.wait_recv()
    n_c, n_d = forward(n_rows, nsend, nrecv)
    n_c.start()
    n_d.start()

    def second_here(k):
        s = lax.rem(ctx + k + 1, CTX)
        remote(
            send2.at[0], llm_rows.at[x, :, :, cols(s)], s2.at[k], r2.at[s], (dp, s)
        ).wait_recv()

    loop(CTX - 1, second_here)
    own2.wait()

    l_a = remote(llm_rows.at[x], llm_rows.at[x], lsend.at[0], lrecv.at[0], to_right)
    l_b = remote(llm_rows.at[x], llm_rows.at[x], lsend.at[1], lrecv.at[1], to_left)
    l_a.start()
    l_b.start()

    for c in w_copies:
        c.wait_recv()
    w_shares = [
        remote(w1_all.at[1, mine], w1_all.at[1, mine], wsend.at[3], wrecv.at[3], sibling),
        remote(w2_all.at[1, mine], w2_all.at[1, mine], wsend.at[4], wrecv.at[4], sibling),
    ]
    for c in w_shares:
        c.start()

    l_a.wait_recv()
    l_b.wait_recv()
    l_c, l_d = forward(llm_rows, lsend, lrecv)
    l_c.start()
    l_d.start()

    for c in w_shares:
        c.wait_recv()
    n_c.wait_recv()
    n_d.wait_recv()
    l_c.wait_recv()
    l_d.wait_recv()
    n_here.wait()
    for c in keep_w:
        c.wait()
    for c in [n_a, n_b, n_c, n_d, l_a, l_b, l_c, l_d] + w_copies + w_shares:
        c.wait_send()

    def sent(k):
        first(k).wait_send()
        second(k).wait_send()

    loop(CTX - 1, sent)


def gather_rows(inv, order, frames, llm, vit, gain, bias, w1, w2):
    any_, vmem, smem = (pl.BlockSpec(memory_space=m) for m in (pl.ANY, pltpu.VMEM, pltpu.SMEM))
    dma = pltpu.SemaphoreType.DMA
    return pl.pallas_call(
        gather_kernel,
        out_shape=(
            jax.ShapeDtypeStruct((X, 2, 64, 4096), BF16),
            jax.ShapeDtypeStruct((X, 2, 64, 2560), BF16),
            jax.ShapeDtypeStruct((2, 320, 2560), BF16),
            jax.ShapeDtypeStruct((2, 320, 4096), BF16),
            jax.ShapeDtypeStruct((2, 8, 320), F32),
        ),
        in_specs=[smem, smem, smem, vmem, vmem, vmem, any_, any_, any_],
        out_specs=[any_] * 5,
        scratch_shapes=[
            pltpu.VMEM((2, 64, 4096), BF16),
            pltpu.VMEM((2, 64, 2560), BF16),
            pltpu.VMEM((CTX, 2, 64, 128), BF16),
            pltpu.VMEM((CTX, 2, 64, 128), BF16),
            dma((CTX,)), dma((CTX,)), dma((CTX,)), dma((CTX,)),
            dma((6,)), dma((5,)), dma((5,)), dma((4,)), dma((4,)), dma((4,)), dma((4,)),
        ],
        compiler_params=pltpu.CompilerParams(
            collective_id=0, has_side_effects=True, vmem_limit_bytes=40 * 2**20
        ),
        name="gather_rows",
    )(inv, order, frames, llm, vit, gain, bias, w1, w2)


def ring_sum(n, me, own, halves, bufs, accs, send, recv, to, finish):
    half = n // 2
    copies = []
    for d, sign in enumerate((1, -1)):
        t = lax.rem(me + n + sign * half, n)
        at = pl.ds(*halves[d])
        c = remote(own(t).at[at], bufs.at[d, 0, at], send.at[d, 0], recv.at[d, 0], to[d])
        c.start()
        copies.append(c)
    last = list(copies)
    yield
    for s in range(2, half + 1):
        for d, sign in enumerate((1, -1)):
            last[d].wait_recv()
            t = lax.rem(me + n + sign * (half + 1 - s), n)
            mine, came, out = own(t), bufs.at[d, s - 2], accs.at[d, s - 2]

            def add(i, mine=mine, came=came, out=out):
                out[i] = (mine[i].astype(F32) + came[i].astype(F32)).astype(BF16)

            def carry(i, mine=mine, out=out):
                out[i] = mine[i]

            if len(out.shape) == 2:
                if s == 2:
                    (a, an), (b, bn) = halves[d], halves[1 - d]
                    out[pl.ds(a, an)] = (
                        mine[pl.ds(a, an)].astype(F32) + came[pl.ds(a, an)].astype(F32)
                    ).astype(BF16)
                    out[pl.ds(b, bn)] = mine[pl.ds(b, bn)]
                else:
                    out[...] = (mine[...].astype(F32) + came[...].astype(F32)).astype(BF16)
            elif s == 2:
                (a, an), (b, bn) = halves[d], halves[1 - d]
                loop(an, lambda i, add=add, a=a: add(a + i))
                loop(bn, lambda i, carry=carry, b=b: carry(b + i))
            else:
                loop(out.shape[0], add)
            c = remote(out, bufs.at[d, s - 1], send.at[d, s - 1], recv.at[d, s - 1], to[d])
            c.start()
            copies.append(c)
            last[d] = c
        yield
    for d in range(2):
        last[d].wait_recv()
    finish(own(me), bufs.at[0, half - 1], bufs.at[1, half - 1])
    for c in copies:
        c.wait_send()


def scatter_kernel(
    ng, g1, g2, vit, gain,
    out_v, out1, out2,
    c1, c2, t1, t2, m1, m2, f1, f2, q1, q2,
    xb, xa, yb2, ya2, zb1, za1, zb2, za2, yb1, ya1,
    csend, crecv, xs, xr, ys2, yr2, zs1, zr1, zs2, zr2, ys1, yr1, qs, qr,
):
    x, y, z, core = place()
    x_to = [device(lax.rem(x + 1, X), y, z, core), device(lax.rem(x + X - 1, X), y, z, core)]
    y_to = [device(x, lax.rem(y + 1, Y), z, core), device(x, lax.rem(y + Y - 1, Y), z, core)]
    z_to = [device(x, y, lax.rem(z + 1, Z), core), device(x, y, lax.rem(z + Z - 1, Z), core)]
    sibling = device(x, y, z, 1 - core)
    z_lo = lax.rem(z, 2)
    swap = device(x, y, z + 1 - 2 * z_lo, 1 - core)
    barrier = greet(x_to + y_to + z_to + [sibling, swap])
    pl.semaphore_wait(barrier, 8)

    def finish_x(own, a, b):
        def rows(i):
            at = pl.ds(pl.multiple_of(i * 16, 16), 16)
            for block in range(2):
                for seg in range(4):
                    cols = slice(seg * SEG, (seg + 1) * SEG)
                    grad = (
                        own[block, at, cols].astype(F32)
                        + a[block, at, cols].astype(F32)
                        + b[block, at, cols].astype(F32)
                    )
                    states = vit[block, at, cols].astype(F32)
                    inv_rms = lax.rsqrt(jnp.mean(states * states, axis=-1, keepdims=True) + EPS)
                    scaled = states * inv_rms
                    g = grad * gain[...]
                    out_v[block, at, cols] = (
                        inv_rms * (g - scaled * jnp.mean(g * scaled, axis=-1, keepdims=True))
                    ).astype(BF16)

        loop(4, rows)

    xg = ring_sum(X, x, lambda t: ng.at[t], ((0, 1), (1, 1)), xb, xa, xs, xr, x_to, finish_x)
    next(xg)

    mine = lax.rem(z_lo + core, 2)
    pairs = []
    for k in range(4):
        yy = lax.rem(y + 2 + k, Y)
        pairs.append(remote(g2.at[1 - mine, yy], c2.at[yy], csend.at[k], crecv.at[k], sibling))
    pairs.append(remote(g1.at[1 - mine], c1, csend.at[4], crecv.at[4], sibling))
    for c in (pairs[0], pairs[4], pairs[1], pairs[2], pairs[3]):
        c.start()

    def fold2(k):
        yy = lax.rem(y + 2 + k, Y)
        pairs[k].wait_recv()

        def add(i):
            t2[yy, i] = (g2[mine, yy, i].astype(F32) + c2[yy, i].astype(F32)).astype(BF16)

        loop(Z, add)

    def fold1():
        pairs[4].wait_recv()

        def add(i):
            yy, zz = i // Z, lax.rem(i, Z)
            t1[zz, yy] = (g1[mine, yy, zz].astype(F32) + c1[yy, zz].astype(F32)).astype(BF16)

        loop(Y * Z, add)

    def keep2(own, a, b):
        def add(i):
            m2[i] = (own[i].astype(F32) + a[i].astype(F32) + b[i].astype(F32)).astype(BF16)

        loop(Z, add)

    def keep1(own, a, b):
        def add(i):
            m1[i] = (own[i].astype(F32) + a[i].astype(F32) + b[i].astype(F32)).astype(BF16)

        loop(Y, add)

    def last2(own, a, b):
        f2[...] = own[...].astype(F32) + a[...].astype(F32) + b[...].astype(F32)

    def last1(own, a, b):
        f1[...] = own[...].astype(F32) + a[...].astype(F32) + b[...].astype(F32)

    fold2(0)
    y2 = ring_sum(Y, y, lambda t: t2.at[t], ((0, 4), (4, 4)), yb2, ya2, ys2, yr2, y_to, keep2)
    next(y2)
    fold1()
    z1 = ring_sum(Z, z, lambda t: t1.at[t], ((0, 2), (2, 2)), zb1, za1, zs1, zr1, z_to, keep1)
    next(z1)
    for k in (1, 2, 3):
        fold2(k)
    next(z1)
    next(xg)
    next(z1)
    next(y2)
    next(z1)
    for _ in z1:
        pass
    y1 = ring_sum(Y, y, lambda t: m1.at[t], ((0, 48), (48, 32)), yb1, ya1, ys1, yr1, y_to, last1)
    next(y1)
    for _ in y2:
        pass
    z2 = ring_sum(Z, z, lambda t: m2.at[t], ((0, 64), (64, 64)), zb2, za2, zs2, zr2, z_to, last2)
    next(z2)
    next(y1)
    for _ in xg:
        pass
    next(z2)
    for _ in y1:
        pass
    for _ in z2:
        pass

    away = core != z_lo

    @pl.when(away)
    def _():
        q1[0] = f1[...].astype(BF16)
        q2[0] = f2[...].astype(BF16)
        a = remote(q1.at[0], q1.at[1], qs.at[0], qr.at[0], swap)
        b = remote(q2.at[0], q2.at[1], qs.at[1], qr.at[1], swap)
        a.start()
        b.start()
        a.wait()
        b.wait()
        out1[...] = q1[1].astype(F32)
        out2[...] = q2[1].astype(F32)

    @pl.when(jnp.logical_not(away))
    def _():
        out1[...] = f1[...]
        out2[...] = f2[...]

    for c in pairs:
        c.wait_send()


def scatter_sums(ng, g1, g2, vit, gain):
    vmem = pl.BlockSpec(memory_space=pltpu.VMEM)
    dma = pltpu.SemaphoreType.DMA
    v = pltpu.VMEM
    n = 320
    sems = []
    for steps in ((5,), (2, 2), (2, 2), (2, 4), (2, 4), (2, 2), (2,)):
        sems += [dma(steps), dma(steps)]
    return pl.pallas_call(
        scatter_kernel,
        out_shape=(
            jax.ShapeDtypeStruct((2, 64, 2560), BF16),
            jax.ShapeDtypeStruct((80, n), F32),
            jax.ShapeDtypeStruct((128, n), F32),
        ),
        in_specs=[vmem] * 5,
        out_specs=[vmem] * 3,
        scratch_shapes=[
            v((Y, Z, 80, n), BF16), v((Y, Z, 128, n), BF16),
            v((Z, Y, 80, n), BF16), v((Y, Z, 128, n), BF16),
            v((Y, 80, n), BF16), v((Z, 128, n), BF16),
            v((80, n), F32), v((128, n), F32),
            v((2, 80, n), BF16), v((2, 128, n), BF16),
            v((2, 2, 2, 64, 2560), BF16), v((2, 1, 2, 64, 2560), BF16),
            v((2, 2, Z, 128, n), BF16), v((2, 1, Z, 128, n), BF16),
            v((2, 4, Y, 80, n), BF16), v((2, 3, Y, 80, n), BF16),
            v((2, 4, 128, n), BF16), v((2, 3, 128, n), BF16),
            v((2, 2, 80, n), BF16), v((2, 1, 80, n), BF16),
        ] + sems,
        compiler_params=pltpu.CompilerParams(
            collective_id=1, has_side_effects=True, vmem_limit_bytes=56 * 2**20
        ),
        name="scatter_sums",
    )(ng, g1, g2, vit, gain)


def body(vit_states, norm_gain, w_first, b_first, w_second, llm_grad, block_order, frame_tokens):
    positions = jnp.arange(64, dtype=jnp.int32)
    matches = (block_order[None, :] == positions[:, None]).astype(jnp.int32)
    inverse = jnp.sum(matches * positions[None, :], axis=1)
    gain = norm_gain.reshape(1, SEG)
    llm_rows, n_rows, w1, w2, b = gather_rows(
        inverse, block_order, frame_tokens, llm_grad.reshape(2, 64, 4096), vit_states[0], gain,
        jnp.broadcast_to(b_first[None, :], (8, 320)), w_first, w_second,
    )
    grads = llm_rows.reshape(512, 4096)
    inputs = n_rows.reshape(512, 2560)
    contract_cols = (((1,), (1,)), ((), ()))
    contract_rows = (((0,), (0,)), ((), ()))
    dot = functools.partial(lax.dot_general, preferred_element_type=F32)
    first, second, ng = [], [], 0.0
    for h in range(2):
        pre_act = dot(inputs, w1[h], contract_cols) + b[h, :1]
        activated = gelu_value(pre_act).astype(BF16)
        hidden_grad = dot(grads, w2[h], contract_cols)
        pre_grad = (hidden_grad * gelu_slope(pre_act)).astype(BF16)
        second.append(dot(grads, activated, contract_rows).astype(BF16))
        first.append(dot(inputs, pre_grad, contract_rows).astype(BF16))
        ng = ng + dot(pre_grad, w1[h], (((1,), (0,)), ((), ())))
    g1 = jnp.stack(first).reshape(2, Y, Z, 80, 320)
    g2 = jnp.stack(second).reshape(2, Y, Z, 128, 320)
    vit_grad, first_grad, second_grad = scatter_sums(
        ng.astype(BF16).reshape(X, 2, 64, 2560), g1, g2, vit_states.reshape(2, 64, 2560), gain
    )
    return (vit_grad.reshape(1, ROWS, 2560), first_grad.T, second_grad.T)


def solution(mesh):
    placed = (
        P("dp", "ctx", None), P(), P("dp", None), P("dp"), P("dp", None), P("dp", "ctx", None), P(), P(),
    )
    return jax.shard_map(
        body,
        mesh=mesh,
        in_specs=placed,
        out_specs=(P("dp", "ctx", None), P("dp", "ctx"), P("dp", "ctx")),
        check_vma=False,
    )
```

```python
import functools
import math

import jax
import jax.numpy as jnp
from jax import lax
from jax.experimental import pallas as pl
from jax.experimental.pallas import tpu as pltpu
from jax.sharding import PartitionSpec as P

MESH = pl.DeviceIdType.MESH
EPS = 1e-06
X, Y, Z, CTX = 4, 4, 8, 32
ROWS, SEG, HID, LLM, VIT = 128, 640, 320, 4096, 2560
HALF = LLM // 2
F32, BF16 = jnp.float32, jnp.bfloat16
NT = (((1,), (1,)), ((), ()))
NN = (((1,), (0,)), ((), ()))
TN = (((0,), (0,)), ((), ()))
dot = functools.partial(lax.dot_general, preferred_element_type=F32)


def place():
    dp, ctx = lax.axis_index("dp"), lax.axis_index("ctx")
    x, y, core = lax.rem(dp, X), ctx // 8, lax.rem(ctx, 2)
    z = lax.rem(ctx // 2, 4) * 2 + dp // X
    return x, y, z, core


def device(x, y, z, core):
    return (lax.rem(z, 2) * X + x, y * 8 + (z // 2) * 2 + core)


def remote(src, dst, send, recv, to):
    return pltpu.make_async_remote_copy(
        src_ref=src, dst_ref=dst, send_sem=send, recv_sem=recv, device_id=to, device_id_type=MESH
    )


def loop(n, body):
    lax.fori_loop(0, n, lambda i, c: (body(i), c)[1], 0)


def part(i, size):
    return pl.ds(pl.multiple_of(i * size, size), size)


def ring_sum(n, me, own, halves, step, bufs, accs, send, recv, to, finish):
    half = n // 2
    copies = []
    for d, sign in enumerate((1, -1)):
        t = lax.rem(me + n + sign * half, n)
        at = pl.ds(*halves[d])
        c = remote(own(t).at[at], bufs.at[d, 0, at], send.at[d, 0], recv.at[d, 0], to[d])
        c.start()
        copies.append(c)
    last = list(copies)
    yield
    for s in range(2, half + 1):
        for d, sign in enumerate((1, -1)):
            t = lax.rem(me + n + sign * (half + 1 - s), n)
            mine, came, out = own(t), bufs.at[d, s - 2], accs.at[d, s - 2]

            def add(first, count, came=came, mine=mine, out=out):
                def one(i):
                    at = pl.ds(pl.multiple_of(first + i * step, step), step)
                    out[at] = (mine[at].astype(F32) + came[at].astype(F32)).astype(BF16)

                loop(count // step, one)

            def carry(first, count, mine=mine, out=out):
                def one(i):
                    at = pl.ds(pl.multiple_of(first + i * step, step), step)
                    out[at] = mine[at]

                loop(count // step, one)

            if s == 2:
                carry(*halves[1 - d])
                last[d].wait_recv()
                add(*halves[d])
            else:
                last[d].wait_recv()
                add(0, out.shape[0])
            c = remote(out, bufs.at[d, s - 1], send.at[d, s - 1], recv.at[d, s - 1], to[d])
            c.start()
            copies.append(c)
            last[d] = c
        yield
    for d in range(2):
        last[d].wait_recv()
    finish(own(me), bufs.at[0, half - 1], bufs.at[1, half - 1])
    for c in copies:
        c.wait_send()


def kernel(
    inv, order, frames, llm, vit, gain, bias, w1, w2,
    out_v, out1, out2,
    masked, recv1a, recv1b, send2, n_rows, l_rows, w1v, w2v, bv,
    pre, hg, act, pg, ng,
    g1, c1, t1, g2, c2, t2,
    m1, m2, f1, f2, q1, q2,
    xb, xa, y1b, y1a, z1b, z1a, z2b, z2a, y2b, y2a,
    s1, r1, s2, r2, loc, wsend, wrecv, nsend, nrecv, lsend, lrecv, esend, erecv,
    xs, xr, y1s, y1r, z1s, z1r, z2s, z2r, y2s, y2r, qs, qr,
):
    recv1 = (recv1a, recv1b)
    x, y, z, core = place()
    ctx, dp = lax.axis_index("ctx"), lax.axis_index("dp")
    right, left, far = lax.rem(x + 1, X), lax.rem(x + X - 1, X), lax.rem(x + 2, X)
    up, down = lax.rem(z + 1, Z), lax.rem(z + Z - 1, Z)
    x_to = [device(right, y, z, core), device(left, y, z, core)]
    y_to = [device(x, lax.rem(y + 1, Y), z, core), device(x, lax.rem(y + Y - 1, Y), z, core)]
    z_to = [device(x, y, up, core), device(x, y, down, core)]
    sibling = device(x, y, z, 1 - core)
    z_lo, z_hi = lax.rem(z, 2), z // 2
    swap = device(x, y, z + 1 - 2 * z_lo, 1 - core)

    barrier = pltpu.get_barrier_semaphore()

    def hello(k):
        pl.semaphore_signal(
            barrier, inc=1, device_id=(dp, lax.rem(ctx + k + 1, CTX)), device_id_type=MESH
        )

    loop(CTX - 1, hello)
    for other in x_to + z_to + [swap]:
        pl.semaphore_signal(barrier, inc=1, device_id=other, device_id_type=MESH)

    keep_w = [
        pltpu.make_async_copy(w1, w1v.at[pl.ds(0, HID)], loc.at[0]),
        pltpu.make_async_copy(w2, w2v.at[pl.ds(0, HID)], loc.at[1]),
        pltpu.make_async_copy(bias, bv.at[pl.ds(0, HID)], loc.at[2]),
    ]
    for c in keep_w:
        c.start()

    def norm(i):
        rows = part(i, 32)
        for seg in range(4):
            cols = slice(seg * SEG, (seg + 1) * SEG)
            states = vit[rows, cols].astype(F32)
            inv_rms = lax.rsqrt(jnp.mean(states * states, axis=-1, keepdims=True) + EPS)
            n_rows[x, rows, cols] = (states * inv_rms * gain[...]).astype(BF16)

    loop(4, norm)

    t0 = order[2 * ctx]
    t1_ = order[2 * ctx + 1]
    low_first = lax.rem(t0 // 4, 4) < 2
    for b in range(2):
        at_first = low_first if b == 0 else jnp.logical_not(low_first)
        index = jnp.where(at_first, 0, 1)
        t = jnp.where(at_first, t0, t1_)
        for frame in range(2):
            count = frames[dp, 2 * t + frame]
            keep = lax.broadcasted_iota(jnp.int32, (32, 512), 0) < count
            rows = pl.ds(32 * frame, 32)

            def mask(c, b=b, index=index, keep=keep, rows=rows):
                cols = part(c, 512)
                masked[b, rows, cols] = jnp.where(
                    keep, llm[index, rows, cols].astype(F32), 0.0
                ).astype(BF16)

            loop(8, mask)

    pl.semaphore_wait(barrier, CTX - 1 + 5)

    def spread(rows, cols, send, recv):
        own = rows.at[x, :, cols]
        return [remote(own, own, send.at[d], recv.at[d], x_to[d]) for d in range(2)]

    def forward(rows, cols, send, recv):
        out = []
        for d, slot in enumerate((left, right)):
            piece = rows.at[slot, pl.ds(64 * d, 64), cols]
            out.append(remote(piece, piece, send.at[2 + d], recv.at[2 + d], x_to[d]))
        return out

    def start(copies):
        for c in copies:
            c.start()

    def received(copies):
        for c in copies:
            c.wait_recv()

    all_n = pl.ds(0, VIT)
    n_a = spread(n_rows, all_n, nsend, nrecv)
    start(n_a)

    def q_of(m):
        return (m // 8) * 4 + lax.rem(m, 4)

    def b_of(m):
        return lax.rem(m // 4, 2)

    q = q_of(ctx)

    def strip(h, k):
        return pl.ds(pl.multiple_of(h * HALF + k * 128, 128), 128)

    def first(h, k):
        m = lax.rem(ctx + k + 1, CTX)
        return remote(
            masked.at[b_of(m), :, strip(h, q_of(m))], recv1[h].at[ctx], s1.at[h, k], r1.at[h, ctx], (dp, m)
        )

    def first_here(h, k):
        s = lax.rem(ctx + k + 1, CTX)
        return remote(masked.at[0, :, strip(h, 0)], recv1[h].at[s], s1.at[h, k], r1.at[h, s], (dp, s))

    own1 = [
        pltpu.make_async_copy(masked.at[b_of(ctx), :, strip(h, q)], recv1[h].at[ctx], loc.at[3 + h])
        for h in range(2)
    ]
    for h in range(2):
        loop(CTX - 1, lambda k, h=h: first(h, k).start())
        own1[h].start()

    def owner(e):
        return (e // 4) * 8 + b_of(ctx) * 4 + lax.rem(e, 4)

    def pick(h, e):
        for i in range(2):
            block = inv[2 * owner(e) + i]
            send2[h, e, pl.ds(64 * i, 64)] = recv1[h][block // 2]

    def second(h, k):
        e = lax.rem(q + k + 1, 16)
        return remote(
            send2.at[h, e], l_rows.at[x, :, strip(h, q)], s2.at[h, k], r2.at[h, q], (dp, owner(e))
        )

    def second_here(h, k):
        e = lax.rem(q + k + 1, 16)
        return remote(
            send2.at[h, e], l_rows.at[x, :, strip(h, e)], s2.at[h, k], r2.at[h, e], (dp, owner(e))
        )

    own2 = [
        pltpu.make_async_copy(send2.at[h, q], l_rows.at[x, :, strip(h, q)], loc.at[5 + h])
        for h in range(2)
    ]

    def reorder(h):
        loop(CTX - 1, lambda k: first_here(h, k).wait_recv())
        own1[h].wait()

        def send(k):
            pick(h, lax.rem(q + k + 1, 16))
            second(h, k).start()

        loop(15, send)
        pick(h, q)
        own2[h].start()

    def reordered(h):
        loop(15, lambda k: second_here(h, k).wait_recv())
        own2[h].wait()

    to_z = device(x, y, jnp.where(core == 0, up, down), core)
    mine_w = pl.ds(pl.multiple_of(core * 160, 32), 160)
    there_w = pl.ds(pl.multiple_of(HID + core * 160, 32), 160)
    other_w = pl.ds(HID, HID)
    w_a = [
        remote(w1.at[mine_w], w1v.at[there_w], wsend.at[0], wrecv.at[0], to_z),
        remote(bias, bv.at[other_w], wsend.at[1], wrecv.at[1], to_z),
    ]
    w_b = [remote(w2.at[mine_w], w2v.at[there_w], wsend.at[2], wrecv.at[2], to_z)]
    w_c = [remote(w1v.at[there_w], w1v.at[there_w], wsend.at[3], wrecv.at[3], sibling)]
    w_d = [remote(w2v.at[there_w], w2v.at[there_w], wsend.at[4], wrecv.at[4], sibling)]

    def group(k):
        return pl.ds(k * HID, HID)

    def activate(k):
        pre[group(k)] = dot(w1v[group(k)], n_rows[...].reshape(X * ROWS, VIT), NT)

        def chunk(i):
            at = pl.ds(pl.multiple_of(k * HID + i * 32, 32), 32)
            v = pre[at] + bv[at, :1]
            cdf = 0.5 * (1.0 + lax.erf(v * (1.0 / math.sqrt(2.0))))
            density = jnp.exp(-0.5 * v * v) * (1.0 / math.sqrt(2.0 * math.pi))
            act[at] = (v * cdf).astype(BF16)
            pre[at] = cdf + v * density

        loop(10, chunk)

    def tokens(slot):
        return part(slot, ROWS)

    def hidden(slot, h, k):
        cols = pl.ds(h * HALF, HALF)
        got = dot(w2v[group(k), cols], l_rows[slot, :, cols], NT)
        if h == 0:
            hg[group(k), tokens(slot)] = got
        else:
            hg[group(k), tokens(slot)] += got

    def gradient(slot):
        def chunk(i):
            at = part(i, 64)
            pg[at, tokens(slot)] = (hg[at, tokens(slot)] * pre[at, tokens(slot)]).astype(BF16)

        loop(10, chunk)
        for c in range(2):
            cols = slice(c * 1280, (c + 1) * 1280)
            ng[slot, :, cols] = dot(pg[:, tokens(slot)], w1v[:, cols], TN).astype(BF16)

    mine = lax.rem(z_lo + core, 2)
    own_h, other_h = (pl.ds(pl.multiple_of(k * HID, HID), HID) for k in (mine, 1 - mine))

    def second_grad(h, at, into):
        for c in range(4):
            cols = slice(h * HALF + c * 512, h * HALF + (c + 1) * 512)
            got = dot(act[at], l_rows[:, :, cols].reshape(X * ROWS, 512), NN).astype(BF16)
            for i in range(4):
                into[h, (4 * c + i) % Z, c // 2] = got[:, i * 128 : (i + 1) * 128]

    def first_grad(at, into):
        for yy in range(Y):
            got = dot(pg[at], n_rows[:, :, yy * SEG : (yy + 1) * SEG].reshape(X * ROWS, SEG), NN)
            into[yy] = got.astype(BF16)

    e2 = [remote(g2.at[h], c2.at[h], esend.at[h], erecv.at[h], sibling) for h in range(2)]
    e1 = remote(g1, c1, esend.at[2], erecv.at[2], sibling)

    def fold2(h):
        e2[h].wait_recv()

        def add(i):
            at = (h, i // 2, lax.rem(i, 2))
            t2[at] = (t2[at].astype(F32) + c2[at].astype(F32)).astype(BF16)

        loop(2 * Z, add)

    def fold1():
        e1.wait_recv()

        def add(i):
            at = (i // 5, part(lax.rem(i, 5), 64))
            t1[at] = (t1[at].astype(F32) + c1[at].astype(F32)).astype(BF16)

        loop(5 * Y, add)

    def keep2(h):
        def finish(own, a, b):
            for i in range(2):
                m2[2 * h + i] = (
                    own[i].astype(F32) + a[i].astype(F32) + b[i].astype(F32)
                ).astype(BF16)

        return finish

    def keep1(own, a, b):
        for c in range(5):
            cols = slice(c * 128, (c + 1) * 128)
            total = own[:, cols].astype(F32) + a[:, cols].astype(F32) + b[:, cols].astype(F32)
            m1[cols] = total.T.astype(BF16)

    def last(f):
        def finish(own, a, b):
            f[...] = own[...].astype(F32) + a[...].astype(F32) + b[...].astype(F32)

        return finish

    def finish_x(own, a, b):
        def rows(i):
            at = part(i, 16)
            for seg in range(4):
                cols = slice(seg * SEG, (seg + 1) * SEG)
                grad = (
                    own[at, cols].astype(F32) + a[at, cols].astype(F32) + b[at, cols].astype(F32)
                )
                states = vit[at, cols].astype(F32)
                inv_rms = lax.rsqrt(jnp.mean(states * states, axis=-1, keepdims=True) + EPS)
                scaled = states * inv_rms
                g = grad * gain[...]
                out_v[at, cols] = (
                    inv_rms * (g - scaled * jnp.mean(g * scaled, axis=-1, keepdims=True))
                ).astype(BF16)

        loop(8, rows)

    x_ring = ring_sum(
        X, x, lambda t: ng.at[t], ((0, 64), (64, 64)), 16, xb, xa, xs, xr, x_to, finish_x
    )
    z2_rings = [
        ring_sum(
            Z, z, lambda t, h=h: t2.at[h, t], ((0, 1), (1, 1)), 1,
            z2b.at[h], z2a.at[h], z2s.at[h], z2r.at[h], z_to, keep2(h),
        )
        for h in range(2)
    ]
    y2_ring = ring_sum(
        Y, y, lambda t: m2.at[t], ((0, 160), (160, 160)), 160, y2b, y2a, y2s, y2r, y_to, last(f2)
    )
    y1_ring = ring_sum(
        Y, y, lambda t: t1.at[t], ((0, 160), (160, 160)), 32, y1b, y1a, y1s, y1r, y_to, keep1
    )
    z1_ring = ring_sum(
        Z, z, lambda t: m1.at[part(t, 80)], ((0, 48), (48, 32)), 16, z1b, z1a, z1s, z1r, z_to, last(f1)
    )

    def run(*rings):
        for r in rings:
            next(r, None)

    l_cols = [pl.ds(h * HALF, HALF) for h in range(2)]
    l_a = [spread(l_rows, l_cols[h], lsend.at[h], lrecv.at[h]) for h in range(2)]
    l_f = [forward(l_rows, l_cols[h], lsend.at[h], lrecv.at[h]) for h in range(2)]
    n_f = forward(n_rows, all_n, nsend, nrecv)

    reorder(0)
    received(n_a)
    start(n_f)
    start(w_a)
    reorder(1)
    start(w_b)
    reordered(0)
    start(l_a[0])
    received(n_f)
    for c in keep_w:
        c.wait()
    activate(0)
    reordered(1)
    start(l_a[1])
    hidden(x, 0, 0)
    received(l_a[0])
    start(l_f[0])
    received(w_a)
    start(w_c)
    for slot in (left, right):
        hidden(slot, 0, 0)
    hidden(x, 1, 0)
    received(w_c)
    activate(1)
    received(l_a[1])
    start(l_f[1])
    received(l_f[0])
    second_grad(0, other_h, g2)
    e2[0].start()
    second_grad(0, own_h, t2)
    received(w_b)
    start(w_d)
    hidden(far, 0, 0)
    for slot in (left, right):
        hidden(slot, 1, 0)
    fold2(0)
    run(z2_rings[0])
    received(w_d)
    for slot in (x, left, right, far):
        hidden(slot, 0, 1)
    for slot in (x, left, right):
        hidden(slot, 1, 1)
    received(l_f[1])
    hidden(far, 1, 0)
    hidden(far, 1, 1)
    gradient(far)
    run(x_ring)
    run(z2_rings[0])
    gradient(left)
    gradient(right)
    gradient(x)
    first_grad(other_h, g1)
    e1.start()
    second_grad(1, other_h, g2)
    e2[1].start()
    run(x_ring)
    first_grad(own_h, t1)
    run(z2_rings[0])
    second_grad(1, own_h, t2)
    fold1()
    run(y1_ring)
    fold2(1)
    run(z2_rings[1])
    run(z2_rings[0])
    run(z2_rings[1])
    run(y1_ring)
    run(z2_rings[0])
    run(z2_rings[1])
    run(y1_ring)
    run(z1_ring)
    run(z2_rings[1])
    run(z1_ring)
    run(x_ring)
    run(z1_ring)
    run(z2_rings[1])
    run(y2_ring)
    run(z1_ring)
    run(y2_ring)
    run(z1_ring)
    run(y2_ring)

    away = core != z_lo

    @pl.when(away)
    def _():
        q1[0] = f1[...].astype(BF16)
        q2[0] = f2[...].astype(BF16)
        a = remote(q1.at[0], q1.at[1], qs.at[0], qr.at[0], swap)
        b = remote(q2.at[0], q2.at[1], qs.at[1], qr.at[1], swap)
        a.start()
        b.start()
        a.wait()
        b.wait()
        out1[...] = q1[1].astype(F32)
        out2[...] = q2[1].astype(F32)

    @pl.when(jnp.logical_not(away))
    def _():
        out1[...] = f1[...]
        out2[...] = f2[...]

    for c in n_a + n_f + l_a[0] + l_a[1] + l_f[0] + l_f[1] + w_a + w_b + w_c + w_d + e2 + [e1]:
        c.wait_send()
    for h in range(2):
        loop(CTX - 1, lambda k, h=h: first(h, k).wait_send())
        loop(15, lambda k, h=h: second(h, k).wait_send())


def fused(inv, order, frames, llm, vit, gain, bias, w1, w2):
    any_, vmem, smem = (pl.BlockSpec(memory_space=m) for m in (pl.ANY, pltpu.VMEM, pltpu.SMEM))
    dma = pltpu.SemaphoreType.DMA

    def v(*shape, dtype=BF16):
        return pltpu.VMEM(shape, dtype)

    f32 = functools.partial(v, dtype=F32)
    pairs = [(2, CTX), (2, 16)]
    sems = []
    for shape in pairs:
        sems += [dma(shape), dma(shape)]
    sems += [dma((7,))]
    for shape in ((5,), (4,), (2, 4), (3,), (2, 2), (2, 2), (2, 4), (2, 2, 4), (2, 2), (2,)):
        sems += [dma(shape), dma(shape)]
    return pl.pallas_call(
        kernel,
        out_shape=(
            jax.ShapeDtypeStruct((ROWS, VIT), BF16),
            jax.ShapeDtypeStruct((80, HID), F32),
            jax.ShapeDtypeStruct((HID, 128), F32),
        ),
        in_specs=[smem, smem, smem, vmem, vmem, vmem, any_, any_, any_],
        out_specs=[vmem] * 3,
        scratch_shapes=[
            v(2, 64, LLM), v(CTX, 64, 128), v(CTX, 64, 128), v(2, 16, ROWS, 128),
            v(X, ROWS, VIT), v(X, ROWS, LLM),
            v(2 * HID, VIT), v(2 * HID, LLM), f32(2 * HID, 128),
            f32(2 * HID, X * ROWS), f32(2 * HID, X * ROWS),
            v(2 * HID, X * ROWS), v(2 * HID, X * ROWS), v(X, ROWS, VIT),
            v(Y, HID, SEG), v(Y, HID, SEG), v(Y, HID, SEG),
            v(2, Z, 2, HID, 128), v(2, Z, 2, HID, 128), v(2, Z, 2, HID, 128),
            v(SEG, HID), v(Y, HID, 128), f32(80, HID), f32(HID, 128),
            v(2, 80, HID), v(2, HID, 128),
            v(2, 2, ROWS, VIT), v(2, 1, ROWS, VIT),
            v(2, 2, HID, SEG), v(2, 1, HID, SEG),
            v(2, 4, 80, HID), v(2, 3, 80, HID),
            v(2, 2, 4, 2, HID, 128), v(2, 2, 3, 2, HID, 128),
            v(2, 2, HID, 128), v(2, 1, HID, 128),
        ] + sems,
        compiler_params=pltpu.CompilerParams(
            collective_id=0, has_side_effects=True, vmem_limit_bytes=60 * 2**20
        ),
        name="fused",
    )(inv, order, frames, llm, vit, gain, bias, w1, w2)


def body(vit_states, norm_gain, w_first, b_first, w_second, llm_grad, block_order, frame_tokens):
    positions = jnp.arange(64, dtype=jnp.int32)
    matches = (block_order[None, :] == positions[:, None]).astype(jnp.int32)
    inverse = jnp.sum(matches * positions[None, :], axis=1)
    vit_grad, first, second = fused(
        inverse, block_order, frame_tokens, llm_grad.reshape(2, 64, LLM), vit_states[0],
        norm_gain.reshape(1, SEG), jnp.broadcast_to(b_first[:, None], (HID, 128)), w_first, w_second,
    )
    return (vit_grad[None], first.T, second)


def solution(mesh):
    placed = (
        P("dp", "ctx", None), P(), P("dp", None), P("dp"), P("dp", None), P("dp", "ctx", None), P(), P(),
    )
    return jax.shard_map(
        body,
        mesh=mesh,
        in_specs=placed,
        out_specs=(P("dp", "ctx", None), P("dp", "ctx"), P("dp", "ctx")),
        check_vma=False,
    )
```

```python
import functools
import math

import jax
import jax.numpy as jnp
from jax import lax
from jax.experimental import pallas as pl
from jax.experimental.pallas import tpu as pltpu
from jax.sharding import PartitionSpec as P

MESH = pl.DeviceIdType.MESH
EPS = 1e-06
X, Y, Z, CTX = 4, 4, 8, 32
ROWS, SEG, HID, LLM, VIT = 128, 640, 320, 4096, 2560
HALF = LLM // 2
CHUNKS = tuple((h, pl.ds(r, 32)) for h in range(2) for r in (0, 32))
F32, BF16 = jnp.float32, jnp.bfloat16
NT = (((1,), (1,)), ((), ()))
NN = (((1,), (0,)), ((), ()))
TN = (((0,), (0,)), ((), ()))
dot = functools.partial(lax.dot_general, preferred_element_type=F32)


def place():
    dp, ctx = lax.axis_index("dp"), lax.axis_index("ctx")
    x, y, core = lax.rem(dp, X), ctx // 8, lax.rem(ctx, 2)
    z = lax.rem(ctx // 2, 4) * 2 + dp // X
    return x, y, z, core


def device(x, y, z, core):
    return (lax.rem(z, 2) * X + x, y * 8 + (z // 2) * 2 + core)


def remote(src, dst, send, recv, to):
    return pltpu.make_async_remote_copy(
        src_ref=src, dst_ref=dst, send_sem=send, recv_sem=recv, device_id=to, device_id_type=MESH
    )


def loop(n, body):
    lax.fori_loop(0, n, lambda i, c: (body(i), c)[1], 0)


def part(i, size):
    return pl.ds(pl.multiple_of(i * size, size), size)


def ring_sum(n, me, own, halves, step, bufs, accs, send, recv, to, finish):
    half = n // 2
    copies = []
    for d, sign in enumerate((1, -1)):
        t = lax.rem(me + n + sign * half, n)
        at = pl.ds(*halves[d])
        c = remote(own(t).at[at], bufs.at[d, 0, at], send.at[d, 0], recv.at[d, 0], to[d])
        c.start()
        copies.append(c)
    last = list(copies)
    yield
    for s in range(2, half + 1):
        for d, sign in enumerate((1, -1)):
            t = lax.rem(me + n + sign * (half + 1 - s), n)
            mine, came, out = own(t), bufs.at[d, s - 2], accs.at[d, s - 2]

            def add(first, count, came=came, mine=mine, out=out):
                def one(i):
                    at = pl.ds(pl.multiple_of(first + i * step, step), step)
                    out[at] = (mine[at].astype(F32) + came[at].astype(F32)).astype(BF16)

                loop(count // step, one)

            def carry(first, count, mine=mine, out=out):
                def one(i):
                    at = pl.ds(pl.multiple_of(first + i * step, step), step)
                    out[at] = mine[at]

                loop(count // step, one)

            if s == 2:
                carry(*halves[1 - d])
                last[d].wait_recv()
                add(*halves[d])
            else:
                last[d].wait_recv()
                add(0, out.shape[0])
            c = remote(out, bufs.at[d, s - 1], send.at[d, s - 1], recv.at[d, s - 1], to[d])
            c.start()
            copies.append(c)
            last[d] = c
        yield
    for d in range(2):
        last[d].wait_recv()
    finish(own(me), bufs.at[0, half - 1], bufs.at[1, half - 1])
    for c in copies:
        c.wait_send()


def kernel(
    inv, order, frames, llm, vit, gain, bias, w1, w2,
    out_v, out1, out2,
    masked, recv1a, recv1b, recv1c, recv1d, send2a, send2b, send2c, send2d, n_rows, l_rows, w1v, w2v, bv,
    pre, hg, act, pg, ng,
    act_s, pg_s, t1, t2,
    m1, m2, f1, f2, q1, q2,
    xb, xa, y1b, y1a, z1b, z1a, z2b, z2a, y2b, y2a,
    s1, r1, s2, r2, loc, wsend, wrecv, nsend, nrecv, lsend, lrecv, csend, crecv,
    xs, xr, y1s, y1r, z1s, z1r, z2s, z2r, y2s, y2r, qs, qr,
):
    recv1, send2 = (recv1a, recv1b, recv1c, recv1d), (send2a, send2b, send2c, send2d)
    x, y, z, core = place()
    ctx, dp = lax.axis_index("ctx"), lax.axis_index("dp")
    right, left, far = lax.rem(x + 1, X), lax.rem(x + X - 1, X), lax.rem(x + 2, X)
    up, down = lax.rem(z + 1, Z), lax.rem(z + Z - 1, Z)
    x_to = [device(right, y, z, core), device(left, y, z, core)]
    y_to = [device(x, lax.rem(y + 1, Y), z, core), device(x, lax.rem(y + Y - 1, Y), z, core)]
    z_to = [device(x, y, up, core), device(x, y, down, core)]
    sibling = device(x, y, z, 1 - core)
    z_lo, z_hi = lax.rem(z, 2), z // 2
    swap = device(x, y, z + 1 - 2 * z_lo, 1 - core)

    barrier = pltpu.get_barrier_semaphore()

    def hello(k):
        pl.semaphore_signal(
            barrier, inc=1, device_id=(dp, lax.rem(ctx + k + 1, CTX)), device_id_type=MESH
        )

    loop(CTX - 1, hello)
    for other in x_to + z_to + [swap]:
        pl.semaphore_signal(barrier, inc=1, device_id=other, device_id_type=MESH)

    keep_w = [
        pltpu.make_async_copy(w1, w1v.at[pl.ds(0, HID)], loc.at[0]),
        pltpu.make_async_copy(w2, w2v.at[pl.ds(0, HID)], loc.at[1]),
    ]
    for c in keep_w:
        c.start()

    bv[pl.ds(0, HID)] = jnp.broadcast_to(bias[...][None, :], (128, HID)).T

    def norm(i):
        rows = part(i, 32)
        for seg in range(4):
            cols = slice(seg * SEG, (seg + 1) * SEG)
            states = vit[rows, cols].astype(F32)
            inv_rms = lax.rsqrt(jnp.mean(states * states, axis=-1, keepdims=True) + EPS)
            n_rows[0, x, i // 2, part(lax.rem(i, 2), 32), cols] = (
                states * inv_rms * gain[...][None, :]
            ).astype(BF16)

    loop(4, norm)

    t0 = order[2 * ctx]
    t1_ = order[2 * ctx + 1]
    low_first = lax.rem(t0 // 4, 4) < 2
    for b in range(2):
        at_first = low_first if b == 0 else jnp.logical_not(low_first)
        index = jnp.where(at_first, 0, 1)
        t = jnp.where(at_first, t0, t1_)
        for frame in range(2):
            count = frames[dp, 2 * t + frame]
            keep = lax.broadcasted_iota(jnp.int32, (32, 512), 0) < count
            rows = pl.ds(32 * frame, 32)

            def mask(c, b=b, index=index, keep=keep, rows=rows):
                cols = part(c, 512)
                masked[b, rows, cols] = jnp.where(
                    keep, llm[index, rows, cols].astype(F32), 0.0
                ).astype(BF16)

            loop(8, mask)

    pl.semaphore_wait(barrier, CTX - 1 + 5)

    def spread(piece, send, recv):
        own = piece(x, slice(0, 2))
        return [remote(own, own, send.at[d], recv.at[d], x_to[d]) for d in range(2)]

    def forward(piece, send, recv):
        out = []
        for d, slot in enumerate((left, right)):
            one = piece(slot, d)
            out.append(remote(one, one, send.at[2 + d], recv.at[2 + d], x_to[d]))
        return out

    def start(copies):
        for c in copies:
            c.start()

    def received(copies):
        for c in copies:
            c.wait_recv()

    def n_piece(slot, block):
        return n_rows.at[0, slot, block]

    n_a = spread(n_piece, nsend, nrecv)
    n_f = forward(n_piece, nsend, nrecv)

    def q_of(m):
        return (m // 8) * 4 + lax.rem(m, 4)

    def b_of(m):
        return lax.rem(m // 4, 2)

    q = q_of(ctx)

    def strip(h, k):
        return pl.ds(pl.multiple_of(h * HALF + k * 128, 128), 128)

    def first(c, k):
        h, rows = CHUNKS[c]
        m = lax.rem(ctx + k + 1, CTX)
        return remote(
            masked.at[b_of(m), rows, strip(h, q_of(m))], recv1[c].at[ctx], s1.at[c, k], r1.at[c, ctx], (dp, m)
        )

    def first_here(c, k):
        h, rows = CHUNKS[c]
        s = lax.rem(ctx + k + 1, CTX)
        return remote(masked.at[0, rows, strip(h, 0)], recv1[c].at[s], s1.at[c, k], r1.at[c, s], (dp, s))

    own1 = [
        pltpu.make_async_copy(masked.at[b_of(ctx), rows, strip(h, q)], recv1[c].at[ctx], loc.at[2 + c])
        for c, (h, rows) in enumerate(CHUNKS)
    ]

    def offer(c):
        loop(CTX - 1, lambda k: first(c, k).start())
        own1[c].start()

    def owner(e):
        return (e // 4) * 8 + b_of(ctx) * 4 + lax.rem(e, 4)

    def pick(c, e):
        for i in range(2):
            block = inv[2 * owner(e) + i]
            send2[c][e, i] = recv1[c][block // 2]

    def landing(c, k):
        h, rows = CHUNKS[c]
        return l_rows.at[0, x, :, rows, strip(h, k)]

    def second(c, k):
        e = lax.rem(q + k + 1, 16)
        return remote(send2[c].at[e], landing(c, q), s2.at[c, k], r2.at[c, q], (dp, owner(e)))

    def second_here(c, k):
        e = lax.rem(q + k + 1, 16)
        return remote(send2[c].at[e], landing(c, e), s2.at[c, k], r2.at[c, e], (dp, owner(e)))

    own2 = [
        pltpu.make_async_copy(send2[c].at[q], landing(c, q), loc.at[6 + c])
        for c in range(len(CHUNKS))
    ]

    def reorder(c):
        loop(CTX - 1, lambda k: first_here(c, k).wait_recv())
        own1[c].wait()

        def send(k):
            pick(c, lax.rem(q + k + 1, 16))
            second(c, k).start()

        loop(15, send)
        pick(c, q)
        own2[c].start()

    def reordered(c):
        loop(15, lambda k: second_here(c, k).wait_recv())
        own2[c].wait()

    to_z = device(x, y, jnp.where(core == 0, up, down), core)
    y_next, y_prev, y_far = lax.rem(y + 1, Y), lax.rem(y + Y - 1, Y), lax.rem(y + 2, Y)
    w_cols = [pl.ds(pl.multiple_of(core * (n // 2), 128), n // 2) for n in (VIT, LLM)]
    w_in, w_at = (w1, w2), (w1v, w2v)

    def quarter(r, yy, first_row, count):
        return w_at[r].at[pl.ds(pl.multiple_of(HID + yy * 80 + first_row, 16), count), w_cols[r]]

    w_z, w_y, w_f, w_c = [], [[], []], [[], []], []
    for r in range(2):
        own_quarter = w_in[r].at[pl.ds(pl.multiple_of(y * 80, 16), 80), w_cols[r]]
        here = quarter(r, y, 0, 80)
        w_z.append(remote(own_quarter, here, wsend.at[r, 0], wrecv.at[r, 0], to_z))
        for d, (slot, at) in enumerate(((y_prev, (0, 48)), (y_next, (48, 32)))):
            w_y[r].append(remote(here, here, wsend.at[r, 1 + d], wrecv.at[r, 1 + d], y_to[d]))
            piece = quarter(r, slot, *at)
            w_f[r].append(remote(piece, piece, wsend.at[r, 3 + d], wrecv.at[r, 3 + d], y_to[d]))
        share = w_at[r].at[pl.ds(HID, HID), w_cols[r]]
        w_c.append(remote(share, share, wsend.at[r, 5], wrecv.at[r, 5], sibling))
    w_z.append(remote(bv.at[pl.ds(0, HID)], bv.at[pl.ds(HID, HID)], wsend.at[2, 0], wrecv.at[2, 0], to_z))

    def weights_round(r):
        w_z[r].wait_recv()
        start(w_y[r])

    def weights_on(r):
        received(w_y[r])
        start(w_f[r])

    def weights_share(r):
        received(w_f[r])
        w_c[r].start()

    def group(k):
        return pl.ds(k * HID, HID)

    def activate(k):
        pre[group(k)] = dot(w1v[group(k)], n_rows[0].reshape(X * ROWS, VIT), NT)

        def chunk(i):
            at = pl.ds(pl.multiple_of(k * HID + i * 32, 32), 32)
            v = pre[at] + bv[at, :1]
            cdf = 0.5 * (1.0 + lax.erf(v * (1.0 / math.sqrt(2.0))))
            density = jnp.exp(-0.5 * v * v) * (1.0 / math.sqrt(2.0 * math.pi))
            act[at] = (v * cdf).astype(BF16)
            pre[at] = cdf + v * density

        loop(10, chunk)

    def tokens(slot):
        return part(slot, ROWS)

    def hidden(slot, h, k):
        cols = pl.ds(h * HALF, HALF)
        got = dot(w2v[group(k), cols], l_rows[0, slot, :, :, cols].reshape(ROWS, HALF), NT)
        if h == 0:
            hg[group(k), tokens(slot)] = got
        else:
            hg[group(k), tokens(slot)] += got

    def pre_grad(slot):
        def chunk(i):
            at = part(i, 64)
            pg[at, tokens(slot)] = (hg[at, tokens(slot)] * pre[at, tokens(slot)]).astype(BF16)

        loop(10, chunk)

    def gradient(slot):
        for c in range(2):
            cols = slice(c * 1280, (c + 1) * 1280)
            ng[slot, :, cols] = dot(pg[:, tokens(slot)], w1v[:, cols], TN).astype(BF16)

    mine = lax.rem(z_lo + core, 2)
    own_h, other_h = (pl.ds(pl.multiple_of(k * HID, HID), HID) for k in (mine, 1 - mine))

    def share(src, dst, i):
        return remote(src, dst, csend.at[i], crecv.at[i], sibling)

    def share_l(h, rows, slots, i):
        cols = l_cols[h]
        return share(l_rows.at[0, slots, :, rows, cols], l_rows.at[1, slots, :, rows, cols], i)

    l_cols = [pl.ds(h * HALF, HALF) for h in range(2)]
    c_n = share(n_rows.at[0], n_rows.at[1], 0)
    c_act = share(act.at[other_h], act_s, 1)
    slots = (x, left, right, far)
    c_pg = [share(pg.at[other_h, tokens(slot)], pg_s.at[:, tokens(slot)], 9 + i) for i, slot in enumerate(slots)]
    c_l = [share_l(0, slice(0, 64), slice(0, X), 3), share_l(1, slice(0, 32), slice(0, X), 4)]
    c_last = [share_l(1, slice(32, 64), slot, 5 + i) for i, slot in enumerate(slots)]

    def second_grad(h, c):
        cols = slice(h * HALF + c * 512, h * HALF + (c + 1) * 512)
        rows = [l_rows[k, :, :, :, cols].reshape(X * ROWS, 512) for k in range(2)]
        got = (dot(act[own_h], rows[0], NN) + dot(act_s[...], rows[1], NN)).astype(BF16)
        for i in range(4):
            t2[h, (4 * c + i) % Z, c // 2] = got[:, i * 128 : (i + 1) * 128]

    def first_grad(yy):
        cols = part(yy, SEG)
        rows = [n_rows[k, :, :, :, cols].reshape(X * ROWS, SEG) for k in range(2)]
        t1[yy] = (dot(pg[own_h], rows[0], NN) + dot(pg_s[...], rows[1], NN)).astype(BF16)

    def keep2(h):
        def finish(own, a, b):
            for i in range(2):
                m2[2 * h + i] = (
                    own[i].astype(F32) + a[i].astype(F32) + b[i].astype(F32)
                ).astype(BF16)

        return finish

    def keep1(own, a, b):
        for c in range(5):
            cols = slice(c * 128, (c + 1) * 128)
            total = own[:, cols].astype(F32) + a[:, cols].astype(F32) + b[:, cols].astype(F32)
            m1[cols] = total.T.astype(BF16)

    def last(f):
        def finish(own, a, b):
            f[...] = own[...].astype(F32) + a[...].astype(F32) + b[...].astype(F32)

        return finish

    def finish_x(own, a, b):
        def rows(i):
            at = part(i, 16)
            for seg in range(4):
                cols = slice(seg * SEG, (seg + 1) * SEG)
                grad = (
                    own[at, cols].astype(F32) + a[at, cols].astype(F32) + b[at, cols].astype(F32)
                )
                states = vit[at, cols].astype(F32)
                inv_rms = lax.rsqrt(jnp.mean(states * states, axis=-1, keepdims=True) + EPS)
                scaled = states * inv_rms
                g = grad * gain[...][None, :]
                out_v[at, cols] = (
                    inv_rms * (g - scaled * jnp.mean(g * scaled, axis=-1, keepdims=True))
                ).astype(BF16)

        loop(8, rows)

    x_ring = ring_sum(
        X, x, lambda t: ng.at[t], ((0, 64), (64, 64)), 16, xb, xa, xs, xr, x_to, finish_x
    )
    z2_rings = [
        ring_sum(
            Z, z, lambda t, h=h: t2.at[h, t], ((0, 1), (1, 1)), 1,
            z2b.at[h], z2a.at[h], z2s.at[h], z2r.at[h], z_to, keep2(h),
        )
        for h in range(2)
    ]
    y2_ring = ring_sum(
        Y, y, lambda t: m2.at[t], ((0, 160), (160, 160)), 160, y2b, y2a, y2s, y2r, y_to, last(f2)
    )
    y1_ring = ring_sum(
        Y, y, lambda t: t1.at[t], ((0, 160), (160, 160)), 32, y1b, y1a, y1s, y1r, y_to, keep1
    )
    z1_ring = ring_sum(
        Z, z, lambda t: m1.at[part(t, 80)], ((0, 48), (48, 32)), 16, z1b, z1a, z1s, z1r, z_to, last(f1)
    )

    def run(*rings):
        for r in rings:
            next(r, None)

    def l_piece(c):
        h, rows = CHUNKS[c]
        return lambda slot, block: l_rows.at[0, slot, block, rows, l_cols[h]]

    l_a = [spread(l_piece(c), lsend.at[c], lrecv.at[c]) for c in range(4)]
    l_f = [forward(l_piece(c), lsend.at[c], lrecv.at[c]) for c in range(4)]

    start(n_a)
    offer(0)
    start(w_z)
    reorder(0)
    offer(1)
    received(n_a)
    start(n_f)
    reordered(0)
    start(l_a[0])
    reorder(1)
    offer(2)
    weights_round(0)
    weights_round(1)
    received(n_f)
    c_n.start()
    reordered(1)
    start(l_a[1])
    received(l_a[0])
    start(l_f[0])
    reorder(2)
    offer(3)
    weights_on(0)
    weights_on(1)
    for c in keep_w:
        c.wait()
    activate(0)
    received(l_a[1])
    start(l_f[1])
    weights_share(0)
    weights_share(1)
    reordered(2)
    start(l_a[2])
    reorder(3)
    w_c[0].wait_recv()
    w_z[2].wait_recv()
    activate(1)
    c_act.start()
    received(l_a[2])
    start(l_f[2])
    received(l_f[0])
    received(l_f[1])
    c_l[0].start()
    w_c[1].wait_recv()
    for slot in (x, left):
        for k in range(2):
            hidden(slot, 0, k)
    reordered(3)
    start(l_a[3])
    for slot in (right, far):
        for k in range(2):
            hidden(slot, 0, k)
    c_act.wait_recv()
    c_l[0].wait_recv()
    c_n.wait_recv()
    second_grad(0, 0)
    second_grad(0, 1)
    received(l_a[3])
    start(l_f[3])
    start(c_last[:3])
    second_grad(0, 2)
    second_grad(0, 3)
    run(z2_rings[0])
    received(l_f[2])
    c_l[1].start()
    for i in range(3):
        for k in range(2):
            hidden(slots[i], 1, k)
        pre_grad(slots[i])
        c_pg[i].start()
    received(l_f[3])
    c_last[3].start()
    for k in range(2):
        hidden(far, 1, k)
    pre_grad(far)
    c_pg[3].start()
    gradient(far)
    run(x_ring)
    run(z2_rings[0])
    received(c_pg)
    first_grad(y_far)
    run(y1_ring)
    run(z2_rings[0])
    c_l[1].wait_recv()
    received(c_last)
    for c in range(4):
        second_grad(1, c)
    run(z2_rings[1])
    run(z2_rings[0])
    gradient(left)
    gradient(right)
    run(x_ring)
    run(z2_rings[1])
    first_grad(y_next)
    first_grad(y_prev)
    run(y1_ring)
    run(z2_rings[0])
    run(z2_rings[1])
    first_grad(y)
    gradient(x)
    run(z2_rings[1])
    run(y1_ring)
    run(z1_ring)
    run(z2_rings[1])
    run(y2_ring)
    run(z1_ring)
    run(y2_ring)
    run(z1_ring)
    run(y2_ring)

    away = core != z_lo
    home = [remote(q.at[0], q.at[1], qs.at[i], qr.at[i], swap) for i, q in enumerate((q1, q2))]

    @pl.when(away)
    def _():
        q2[0] = f2[...].astype(BF16)
        home[1].start()

    run(z1_ring)
    run(x_ring)
    run(z1_ring)

    @pl.when(away)
    def _():
        q1[0] = f1[...].astype(BF16)
        home[0].start()
        home[1].wait()
        out2[...] = q2[1].astype(F32)
        home[0].wait()
        out1[...] = q1[1].astype(F32)

    @pl.when(jnp.logical_not(away))
    def _():
        out1[...] = f1[...]
        out2[...] = f2[...]

    for c in n_a + n_f + sum(l_a + l_f + w_y + w_f, []) + w_z + w_c + c_l + c_last + c_pg + [c_n, c_act]:
        c.wait_send()
    for i in range(4):
        loop(CTX - 1, lambda k, i=i: first(i, k).wait_send())
        loop(15, lambda k, i=i: second(i, k).wait_send())


def fused(inv, order, frames, llm, vit, gain, bias, w1, w2):
    any_, vmem, smem = (pl.BlockSpec(memory_space=m) for m in (pl.ANY, pltpu.VMEM, pltpu.SMEM))
    dma = pltpu.SemaphoreType.DMA

    def v(*shape, dtype=BF16):
        return pltpu.VMEM(shape, dtype)

    f32 = functools.partial(v, dtype=F32)
    pairs = [(4, CTX), (4, 16)]
    sems = []
    for shape in pairs:
        sems += [dma(shape), dma(shape)]
    sems += [dma((10,))]
    for shape in ((3, 6), (4,), (4, 4), (13,), (2, 2), (2, 2), (2, 4), (2, 2, 4), (2, 2), (2,)):
        sems += [dma(shape), dma(shape)]
    return pl.pallas_call(
        kernel,
        out_shape=(
            jax.ShapeDtypeStruct((ROWS, VIT), BF16),
            jax.ShapeDtypeStruct((80, HID), F32),
            jax.ShapeDtypeStruct((HID, 128), F32),
        ),
        in_specs=[smem, smem, smem, vmem, vmem, vmem, vmem, any_, any_],
        out_specs=[vmem] * 3,
        scratch_shapes=[
            v(2, 64, LLM), *[v(CTX, 32, 128)] * 4, *[v(16, 2, 32, 128)] * 4,
            v(2, X, 2, 64, VIT), v(2, X, 2, 64, LLM),
            v(2 * HID, VIT), v(2 * HID, LLM), f32(2 * HID, 128),
            f32(2 * HID, X * ROWS), f32(2 * HID, X * ROWS),
            v(2 * HID, X * ROWS), v(2 * HID, X * ROWS), v(X, ROWS, VIT),
            v(HID, X * ROWS), v(HID, X * ROWS),
            v(Y, HID, SEG), v(2, Z, 2, HID, 128),
            v(SEG, HID), v(Y, HID, 128), f32(80, HID), f32(HID, 128),
            v(2, 80, HID), v(2, HID, 128),
            v(2, 2, ROWS, VIT), v(2, 1, ROWS, VIT),
            v(2, 2, HID, SEG), v(2, 1, HID, SEG),
            v(2, 4, 80, HID), v(2, 3, 80, HID),
            v(2, 2, 4, 2, HID, 128), v(2, 2, 3, 2, HID, 128),
            v(2, 2, HID, 128), v(2, 1, HID, 128),
        ] + sems,
        compiler_params=pltpu.CompilerParams(
            collective_id=0, has_side_effects=True, vmem_limit_bytes=60 * 2**20
        ),
        name="fused",
    )(inv, order, frames, llm, vit, gain, bias, w1, w2)


def body(vit_states, norm_gain, w_first, b_first, w_second, llm_grad, block_order, frame_tokens):
    positions = jnp.arange(64, dtype=jnp.int32)
    matches = (block_order[None, :] == positions[:, None]).astype(jnp.int32)
    inverse = jnp.sum(matches * positions[None, :], axis=1)
    vit_grad, first, second = fused(
        inverse, block_order, frame_tokens, llm_grad.reshape(2, 64, LLM), vit_states[0],
        norm_gain, b_first, w_first, w_second,
    )
    return (vit_grad[None], first.T, second)


def solution(mesh):
    placed = (
        P("dp", "ctx", None), P(), P("dp", None), P("dp"), P("dp", None), P("dp", "ctx", None), P(), P(),
    )
    return jax.shard_map(
        body,
        mesh=mesh,
        in_specs=placed,
        out_specs=(P("dp", "ctx", None), P("dp", "ctx"), P("dp", "ctx")),
        check_vma=False,
    )
```

```python
import functools
import math

import jax
import jax.numpy as jnp
from jax import lax
from jax.experimental import pallas as pl
from jax.experimental.pallas import tpu as pltpu
from jax.sharding import PartitionSpec as P

MESH = pl.DeviceIdType.MESH
EPS = 1e-06
X, Y, Z, CTX = 4, 4, 8, 32
ROWS, SEG, HID, LLM, VIT = 128, 640, 320, 4096, 2560
HALF = LLM // 2
CHUNKS = tuple((h, pl.ds(r, 32)) for h in range(2) for r in (0, 32))
F32, BF16 = jnp.float32, jnp.bfloat16
NT = (((1,), (1,)), ((), ()))
NN = (((1,), (0,)), ((), ()))
TN = (((0,), (0,)), ((), ()))
dot = functools.partial(lax.dot_general, preferred_element_type=F32)


def place():
    dp, ctx = lax.axis_index("dp"), lax.axis_index("ctx")
    x, y, core = lax.rem(dp, X), ctx // 8, lax.rem(ctx, 2)
    z = lax.rem(ctx // 2, 4) * 2 + dp // X
    return x, y, z, core


def device(x, y, z, core):
    return (lax.rem(z, 2) * X + x, y * 8 + (z // 2) * 2 + core)


def remote(src, dst, send, recv, to):
    return pltpu.make_async_remote_copy(
        src_ref=src, dst_ref=dst, send_sem=send, recv_sem=recv, device_id=to, device_id_type=MESH
    )


def loop(n, body):
    lax.fori_loop(0, n, lambda i, c: (body(i), c)[1], 0)


def part(i, size):
    return pl.ds(pl.multiple_of(i * size, size), size)


def ring_sum(n, me, own, halves, step, bufs, accs, send, recv, to, finish):
    half = n // 2
    copies = []
    for d, sign in enumerate((1, -1)):
        t = lax.rem(me + n + sign * half, n)
        at = pl.ds(*halves[d])
        c = remote(own(t).at[at], bufs.at[d, 0, at], send.at[d, 0], recv.at[d, 0], to[d])
        c.start()
        copies.append(c)
    last = list(copies)
    yield
    for s in range(2, half + 1):
        for d, sign in enumerate((1, -1)):
            t = lax.rem(me + n + sign * (half + 1 - s), n)
            mine, came, out = own(t), bufs.at[d, s - 2], accs.at[d, s - 2]

            def add(first, count, came=came, mine=mine, out=out):
                def one(i):
                    at = pl.ds(pl.multiple_of(first + i * step, step), step)
                    out[at] = (mine[at].astype(F32) + came[at].astype(F32)).astype(BF16)

                loop(count // step, one)

            def carry(first, count, mine=mine, out=out):
                def one(i):
                    at = pl.ds(pl.multiple_of(first + i * step, step), step)
                    out[at] = mine[at]

                loop(count // step, one)

            if s == 2:
                carry(*halves[1 - d])
                last[d].wait_recv()
                add(*halves[d])
            else:
                last[d].wait_recv()
                add(0, out.shape[0])
            c = remote(out, bufs.at[d, s - 1], send.at[d, s - 1], recv.at[d, s - 1], to[d])
            c.start()
            copies.append(c)
            last[d] = c
        yield
    for d in range(2):
        last[d].wait_recv()
    finish(own(me), bufs.at[0, half - 1], bufs.at[1, half - 1])
    for c in copies:
        c.wait_send()


def kernel(
    inv, order, frames, llm, vit, gain, bias, w1, w2,
    out_v, out1, out2,
    masked, recv1a, recv1b, recv1c, recv1d, send2a, send2b, send2c, send2d, n_rows, l_rows, w1v, w2v, bv,
    pre, hg, act, pg, ng,
    act_s, pg_s, t1, t2,
    m1, m2, f1, f2, q1, q2,
    xb, xa, y1b, y1a, z1b, z1a, z2b, z2a, y2b, y2a,
    s1, r1, s2, r2, loc, wsend, wrecv, nsend, nrecv, lsend, lrecv, csend, crecv,
    xs, xr, y1s, y1r, z1s, z1r, z2s, z2r, y2s, y2r, qs, qr,
):
    recv1, send2 = (recv1a, recv1b, recv1c, recv1d), (send2a, send2b, send2c, send2d)
    x, y, z, core = place()
    ctx, dp = lax.axis_index("ctx"), lax.axis_index("dp")
    right, left, far = lax.rem(x + 1, X), lax.rem(x + X - 1, X), lax.rem(x + 2, X)
    up, down = lax.rem(z + 1, Z), lax.rem(z + Z - 1, Z)
    x_to = [device(right, y, z, core), device(left, y, z, core)]
    y_to = [device(x, lax.rem(y + 1, Y), z, core), device(x, lax.rem(y + Y - 1, Y), z, core)]
    z_to = [device(x, y, up, core), device(x, y, down, core)]
    sibling = device(x, y, z, 1 - core)
    z_lo, z_hi = lax.rem(z, 2), z // 2
    swap = device(x, y, z + 1 - 2 * z_lo, 1 - core)

    barrier = pltpu.get_barrier_semaphore()

    def hello(k):
        pl.semaphore_signal(
            barrier, inc=1, device_id=(dp, lax.rem(ctx + k + 1, CTX)), device_id_type=MESH
        )

    loop(CTX - 1, hello)
    for other in x_to + z_to + [swap]:
        pl.semaphore_signal(barrier, inc=1, device_id=other, device_id_type=MESH)

    keep_w = [
        pltpu.make_async_copy(w1, w1v.at[pl.ds(0, HID)], loc.at[0]),
        pltpu.make_async_copy(w2, w2v.at[pl.ds(0, HID)], loc.at[1]),
    ]
    for c in keep_w:
        c.start()

    bv[pl.ds(0, HID)] = jnp.broadcast_to(bias[...][None, :], (128, HID)).T

    def norm(i):
        rows = part(i, 32)
        for seg in range(4):
            cols = slice(seg * SEG, (seg + 1) * SEG)
            states = vit[rows, cols].astype(F32)
            inv_rms = lax.rsqrt(jnp.mean(states * states, axis=-1, keepdims=True) + EPS)
            n_rows[0, x, i // 2, part(lax.rem(i, 2), 32), cols] = (
                states * inv_rms * gain[...][None, :]
            ).astype(BF16)

    loop(4, norm)

    t0 = order[2 * ctx]
    t1_ = order[2 * ctx + 1]
    low_first = lax.rem(t0 // 4, 4) < 2
    for b in range(2):
        at_first = low_first if b == 0 else jnp.logical_not(low_first)
        index = jnp.where(at_first, 0, 1)
        t = jnp.where(at_first, t0, t1_)
        for frame in range(2):
            count = frames[dp, 2 * t + frame]
            keep = lax.broadcasted_iota(jnp.int32, (32, 512), 0) < count
            rows = pl.ds(32 * frame, 32)

            def mask(c, b=b, index=index, keep=keep, rows=rows):
                cols = part(c, 512)
                masked[b, rows, cols] = jnp.where(
                    keep, llm[index, rows, cols].astype(F32), 0.0
                ).astype(BF16)

            loop(8, mask)

    pl.semaphore_wait(barrier, CTX - 1 + 5)

    def spread(piece, send, recv):
        own = piece(x, slice(0, 2))
        return [remote(own, own, send.at[d], recv.at[d], x_to[d]) for d in range(2)]

    def forward(piece, send, recv):
        out = []
        for d, slot in enumerate((left, right)):
            one = piece(slot, d)
            out.append(remote(one, one, send.at[2 + d], recv.at[2 + d], x_to[d]))
        return out

    def start(copies):
        for c in copies:
            c.start()

    def received(copies):
        for c in copies:
            c.wait_recv()

    def n_piece(slot, block):
        return n_rows.at[0, slot, block]

    n_a = spread(n_piece, nsend, nrecv)
    n_f = forward(n_piece, nsend, nrecv)

    def q_of(m):
        return (m // 8) * 4 + lax.rem(m, 4)

    def b_of(m):
        return lax.rem(m // 4, 2)

    q = q_of(ctx)

    def strip(h, k):
        return pl.ds(pl.multiple_of(h * HALF + k * 128, 128), 128)

    def first(c, k):
        h, rows = CHUNKS[c]
        m = lax.rem(ctx + k + 1, CTX)
        return remote(
            masked.at[b_of(m), rows, strip(h, q_of(m))], recv1[c].at[ctx], s1.at[c, k], r1.at[c, ctx], (dp, m)
        )

    def first_here(c, k):
        h, rows = CHUNKS[c]
        s = lax.rem(ctx + k + 1, CTX)
        return remote(masked.at[0, rows, strip(h, 0)], recv1[c].at[s], s1.at[c, k], r1.at[c, s], (dp, s))

    own1 = [
        pltpu.make_async_copy(masked.at[b_of(ctx), rows, strip(h, q)], recv1[c].at[ctx], loc.at[2 + c])
        for c, (h, rows) in enumerate(CHUNKS)
    ]

    def offer(c):
        loop(CTX - 1, lambda k: first(c, k).start())
        own1[c].start()

    def owner(e):
        return (e // 4) * 8 + b_of(ctx) * 4 + lax.rem(e, 4)

    def pick(c, e):
        for i in range(2):
            block = inv[2 * owner(e) + i]
            send2[c][e, i] = recv1[c][block // 2]

    def landing(c, k):
        h, rows = CHUNKS[c]
        return l_rows.at[0, x, :, rows, strip(h, k)]

    def second(c, k):
        e = lax.rem(q + k + 1, 16)
        return remote(send2[c].at[e], landing(c, q), s2.at[c, k], r2.at[c, q], (dp, owner(e)))

    def second_here(c, k):
        e = lax.rem(q + k + 1, 16)
        return remote(send2[c].at[e], landing(c, e), s2.at[c, k], r2.at[c, e], (dp, owner(e)))

    own2 = [
        pltpu.make_async_copy(send2[c].at[q], landing(c, q), loc.at[6 + c])
        for c in range(len(CHUNKS))
    ]

    def reorder(c):
        loop(CTX - 1, lambda k: first_here(c, k).wait_recv())
        own1[c].wait()

        def send(k):
            pick(c, lax.rem(q + k + 1, 16))
            second(c, k).start()

        loop(15, send)
        pick(c, q)
        own2[c].start()

    def reordered(c):
        loop(15, lambda k: second_here(c, k).wait_recv())
        own2[c].wait()

    to_z = device(x, y, jnp.where(core == 0, up, down), core)
    y_next, y_prev, y_far = lax.rem(y + 1, Y), lax.rem(y + Y - 1, Y), lax.rem(y + 2, Y)
    w_cols = [pl.ds(pl.multiple_of(core * (n // 2), 128), n // 2) for n in (VIT, LLM)]
    w_in, w_at = (w1, w2), (w1v, w2v)

    def quarter(r, yy, first_row, count):
        return w_at[r].at[pl.ds(pl.multiple_of(HID + yy * 80 + first_row, 16), count), w_cols[r]]

    w_z, w_y, w_f, w_c = [], [[], []], [[], []], []
    for r in range(2):
        own_quarter = w_in[r].at[pl.ds(pl.multiple_of(y * 80, 16), 80), w_cols[r]]
        here = quarter(r, y, 0, 80)
        w_z.append(remote(own_quarter, here, wsend.at[r, 0], wrecv.at[r, 0], to_z))
        for d, (slot, at) in enumerate(((y_prev, (0, 48)), (y_next, (48, 32)))):
            w_y[r].append(remote(here, here, wsend.at[r, 1 + d], wrecv.at[r, 1 + d], y_to[d]))
            piece = quarter(r, slot, *at)
            w_f[r].append(remote(piece, piece, wsend.at[r, 3 + d], wrecv.at[r, 3 + d], y_to[d]))
        share = w_at[r].at[pl.ds(HID, HID), w_cols[r]]
        w_c.append(remote(share, share, wsend.at[r, 5], wrecv.at[r, 5], sibling))
    w_z.append(remote(bv.at[pl.ds(0, HID)], bv.at[pl.ds(HID, HID)], wsend.at[2, 0], wrecv.at[2, 0], to_z))

    def weights_round(r):
        w_z[r].wait_recv()
        start(w_y[r])

    def weights_on(r):
        received(w_y[r])
        start(w_f[r])

    def weights_share(r):
        received(w_f[r])
        w_c[r].start()

    def group(k):
        return pl.ds(k * HID, HID)

    def activate(k):
        pre[group(k)] = dot(w1v[group(k)], n_rows[0].reshape(X * ROWS, VIT), NT)

        def chunk(i):
            at = pl.ds(pl.multiple_of(k * HID + i * 32, 32), 32)
            v = pre[at] + bv[at, :1]
            cdf = 0.5 * (1.0 + lax.erf(v * (1.0 / math.sqrt(2.0))))
            density = jnp.exp(-0.5 * v * v) * (1.0 / math.sqrt(2.0 * math.pi))
            act[at] = (v * cdf).astype(BF16)
            pre[at] = cdf + v * density

        loop(10, chunk)

    def tokens(slot):
        return part(slot, ROWS)

    def hidden(slot, h, k):
        cols = pl.ds(h * HALF, HALF)
        got = dot(w2v[group(k), cols], l_rows[0, slot, :, :, cols].reshape(ROWS, HALF), NT)
        if h == 0:
            hg[group(k), tokens(slot)] = got
        else:
            hg[group(k), tokens(slot)] += got

    def pre_grad(slot):
        def chunk(i):
            at = part(i, 64)
            pg[at, tokens(slot)] = (hg[at, tokens(slot)] * pre[at, tokens(slot)]).astype(BF16)

        loop(10, chunk)

    def gradient(slot):
        for c in range(2):
            cols = slice(c * 1280, (c + 1) * 1280)
            ng[slot, :, cols] = dot(pg[:, tokens(slot)], w1v[:, cols], TN).astype(BF16)

    mine = lax.rem(z_lo + core, 2)
    own_h, other_h = (pl.ds(pl.multiple_of(k * HID, HID), HID) for k in (mine, 1 - mine))

    def share(src, dst, i):
        return remote(src, dst, csend.at[i], crecv.at[i], sibling)

    def share_l(h, rows, slots, i):
        cols = l_cols[h]
        return share(l_rows.at[0, slots, :, rows, cols], l_rows.at[1, slots, :, rows, cols], i)

    l_cols = [pl.ds(h * HALF, HALF) for h in range(2)]
    c_n = share(n_rows.at[0], n_rows.at[1], 0)
    c_act = share(act.at[other_h], act_s, 1)
    slots = (x, left, right, far)
    c_pg = [share(pg.at[other_h, tokens(slot)], pg_s.at[:, tokens(slot)], 9 + i) for i, slot in enumerate(slots)]
    c_l = [share_l(0, slice(0, 64), slice(0, X), 3), share_l(1, slice(0, 32), slice(0, X), 4)]
    c_last = [share_l(1, slice(32, 64), slot, 5 + i) for i, slot in enumerate(slots)]

    def second_grad(h, c):
        cols = slice(h * HALF + c * 512, h * HALF + (c + 1) * 512)
        rows = [l_rows[k, :, :, :, cols].reshape(X * ROWS, 512) for k in range(2)]
        got = (dot(act[own_h], rows[0], NN) + dot(act_s[...], rows[1], NN)).astype(BF16)
        for i in range(4):
            t2[h, (4 * c + i) % Z, c // 2] = got[:, i * 128 : (i + 1) * 128]

    def first_grad(yy):
        cols = part(yy, SEG)
        rows = [n_rows[k, :, :, :, cols].reshape(X * ROWS, SEG) for k in range(2)]
        t1[yy] = (dot(pg[own_h], rows[0], NN) + dot(pg_s[...], rows[1], NN)).astype(BF16)

    def keep2(h):
        def finish(own, a, b):
            for i in range(2):
                m2[2 * h + i] = (
                    own[i].astype(F32) + a[i].astype(F32) + b[i].astype(F32)
                ).astype(BF16)

        return finish

    def keep1(own, a, b):
        for c in range(5):
            cols = slice(c * 128, (c + 1) * 128)
            total = own[:, cols].astype(F32) + a[:, cols].astype(F32) + b[:, cols].astype(F32)
            m1[cols] = total.T.astype(BF16)

    def last(f):
        def finish(own, a, b):
            f[...] = own[...].astype(F32) + a[...].astype(F32) + b[...].astype(F32)

        return finish

    def finish_x(own, a, b):
        def rows(i):
            at = part(i, 16)
            for seg in range(4):
                cols = slice(seg * SEG, (seg + 1) * SEG)
                grad = (
                    own[at, cols].astype(F32) + a[at, cols].astype(F32) + b[at, cols].astype(F32)
                )
                states = vit[at, cols].astype(F32)
                inv_rms = lax.rsqrt(jnp.mean(states * states, axis=-1, keepdims=True) + EPS)
                scaled = states * inv_rms
                g = grad * gain[...][None, :]
                out_v[at, cols] = (
                    inv_rms * (g - scaled * jnp.mean(g * scaled, axis=-1, keepdims=True))
                ).astype(BF16)

        loop(8, rows)

    x_ring = ring_sum(
        X, x, lambda t: ng.at[t], ((0, 64), (64, 64)), 16, xb, xa, xs, xr, x_to, finish_x
    )
    z2_rings = [
        ring_sum(
            Z, z, lambda t, h=h: t2.at[h, t], ((0, 1), (1, 1)), 1,
            z2b.at[h], z2a.at[h], z2s.at[h], z2r.at[h], z_to, keep2(h),
        )
        for h in range(2)
    ]
    y2_ring = ring_sum(
        Y, y, lambda t: m2.at[t], ((0, 160), (160, 160)), 160, y2b, y2a, y2s, y2r, y_to, last(f2)
    )
    y1_ring = ring_sum(
        Y, y, lambda t: t1.at[t], ((0, 160), (160, 160)), 32, y1b, y1a, y1s, y1r, y_to, keep1
    )
    z1_ring = ring_sum(
        Z, z, lambda t: m1.at[part(t, 80)], ((0, 48), (48, 32)), 16, z1b, z1a, z1s, z1r, z_to, last(f1)
    )

    def run(*rings):
        for r in rings:
            next(r, None)

    def l_piece(c):
        h, rows = CHUNKS[c]
        return lambda slot, block: l_rows.at[0, slot, block, rows, l_cols[h]]

    l_a = [spread(l_piece(c), lsend.at[c], lrecv.at[c]) for c in range(4)]
    l_f = [forward(l_piece(c), lsend.at[c], lrecv.at[c]) for c in range(4)]

    start(n_a)
    offer(0)
    offer(1)
    reorder(0)
    start(w_z)
    offer(2)
    received(n_a)
    start(n_f)
    reordered(0)
    start(l_a[0])
    reorder(1)
    offer(3)
    weights_round(0)
    weights_round(1)
    received(n_f)
    c_n.start()
    reordered(1)
    start(l_a[1])
    received(l_a[0])
    start(l_f[0])
    reorder(2)
    weights_on(0)
    weights_on(1)
    for c in keep_w:
        c.wait()
    activate(0)
    received(l_a[1])
    start(l_f[1])
    weights_share(0)
    weights_share(1)
    reordered(2)
    start(l_a[2])
    reorder(3)
    w_c[0].wait_recv()
    w_z[2].wait_recv()
    activate(1)
    c_act.start()
    received(l_a[2])
    start(l_f[2])
    received(l_f[0])
    received(l_f[1])
    c_l[0].start()
    w_c[1].wait_recv()
    for slot in (x, left):
        for k in range(2):
            hidden(slot, 0, k)
    reordered(3)
    start(l_a[3])
    for slot in (right, far):
        for k in range(2):
            hidden(slot, 0, k)
    c_act.wait_recv()
    c_l[0].wait_recv()
    c_n.wait_recv()
    second_grad(0, 0)
    second_grad(0, 1)
    received(l_a[3])
    start(l_f[3])
    start(c_last[:3])
    second_grad(0, 2)
    second_grad(0, 3)
    run(z2_rings[0])
    received(l_f[2])
    c_l[1].start()
    for i in range(3):
        for k in range(2):
            hidden(slots[i], 1, k)
        pre_grad(slots[i])
        c_pg[i].start()
    received(l_f[3])
    c_last[3].start()
    for k in range(2):
        hidden(far, 1, k)
    pre_grad(far)
    c_pg[3].start()
    gradient(far)
    run(x_ring)
    run(z2_rings[0])
    received(c_pg)
    first_grad(y_far)
    run(y1_ring)
    run(z2_rings[0])
    c_l[1].wait_recv()
    received(c_last)
    for c in range(4):
        second_grad(1, c)
    run(z2_rings[1])
    run(z2_rings[0])
    gradient(left)
    gradient(right)
    run(x_ring)
    run(z2_rings[1])
    first_grad(y_next)
    first_grad(y_prev)
    run(y1_ring)
    run(z2_rings[0])
    run(z2_rings[1])
    first_grad(y)
    gradient(x)
    run(z2_rings[1])
    run(y1_ring)
    run(z1_ring)
    run(z2_rings[1])
    run(y2_ring)
    run(z1_ring)
    run(z1_ring)
    run(y2_ring)
    run(z1_ring)
    run(y2_ring)

    away = core != z_lo
    home = [remote(q.at[0], q.at[1], qs.at[i], qr.at[i], swap) for i, q in enumerate((q1, q2))]

    @pl.when(away)
    def _():
        q2[0] = f2[...].astype(BF16)
        home[1].start()

    run(z1_ring)

    @pl.when(away)
    def _():
        q1[0] = f1[...].astype(BF16)
        home[0].start()

    run(x_ring)

    @pl.when(away)
    def _():
        home[1].wait()
        out2[...] = q2[1].astype(F32)
        home[0].wait()
        out1[...] = q1[1].astype(F32)

    @pl.when(jnp.logical_not(away))
    def _():
        out1[...] = f1[...]
        out2[...] = f2[...]

    for c in n_a + n_f + sum(l_a + l_f + w_y + w_f, []) + w_z + w_c + c_l + c_last + c_pg + [c_n, c_act]:
        c.wait_send()
    for i in range(4):
        loop(CTX - 1, lambda k, i=i: first(i, k).wait_send())
        loop(15, lambda k, i=i: second(i, k).wait_send())


def fused(inv, order, frames, llm, vit, gain, bias, w1, w2):
    any_, vmem, smem = (pl.BlockSpec(memory_space=m) for m in (pl.ANY, pltpu.VMEM, pltpu.SMEM))
    dma = pltpu.SemaphoreType.DMA

    def v(*shape, dtype=BF16):
        return pltpu.VMEM(shape, dtype)

    f32 = functools.partial(v, dtype=F32)
    pairs = [(4, CTX), (4, 16)]
    sems = []
    for shape in pairs:
        sems += [dma(shape), dma(shape)]
    sems += [dma((10,))]
    for shape in ((3, 6), (4,), (4, 4), (13,), (2, 2), (2, 2), (2, 4), (2, 2, 4), (2, 2), (2,)):
        sems += [dma(shape), dma(shape)]
    return pl.pallas_call(
        kernel,
        out_shape=(
            jax.ShapeDtypeStruct((ROWS, VIT), BF16),
            jax.ShapeDtypeStruct((80, HID), F32),
            jax.ShapeDtypeStruct((HID, 128), F32),
        ),
        in_specs=[smem, smem, smem, vmem, vmem, vmem, vmem, any_, any_],
        out_specs=[vmem] * 3,
        scratch_shapes=[
            v(2, 64, LLM), *[v(CTX, 32, 128)] * 4, *[v(16, 2, 32, 128)] * 4,
            v(2, X, 2, 64, VIT), v(2, X, 2, 64, LLM),
            v(2 * HID, VIT), v(2 * HID, LLM), f32(2 * HID, 128),
            f32(2 * HID, X * ROWS), f32(2 * HID, X * ROWS),
            v(2 * HID, X * ROWS), v(2 * HID, X * ROWS), v(X, ROWS, VIT),
            v(HID, X * ROWS), v(HID, X * ROWS),
            v(Y, HID, SEG), v(2, Z, 2, HID, 128),
            v(SEG, HID), v(Y, HID, 128), f32(80, HID), f32(HID, 128),
            v(2, 80, HID), v(2, HID, 128),
            v(2, 2, ROWS, VIT), v(2, 1, ROWS, VIT),
            v(2, 2, HID, SEG), v(2, 1, HID, SEG),
            v(2, 4, 80, HID), v(2, 3, 80, HID),
            v(2, 2, 4, 2, HID, 128), v(2, 2, 3, 2, HID, 128),
            v(2, 2, HID, 128), v(2, 1, HID, 128),
        ] + sems,
        compiler_params=pltpu.CompilerParams(
            collective_id=0, has_side_effects=True, vmem_limit_bytes=60 * 2**20
        ),
        name="fused",
    )(inv, order, frames, llm, vit, gain, bias, w1, w2)


def body(vit_states, norm_gain, w_first, b_first, w_second, llm_grad, block_order, frame_tokens):
    positions = jnp.arange(64, dtype=jnp.int32)
    matches = (block_order[None, :] == positions[:, None]).astype(jnp.int32)
    inverse = jnp.sum(matches * positions[None, :], axis=1)
    vit_grad, first, second = fused(
        inverse, block_order, frame_tokens, llm_grad.reshape(2, 64, LLM), vit_states[0],
        norm_gain, b_first, w_first, w_second,
    )
    return (vit_grad[None], first.T, second)


def solution(mesh):
    placed = (
        P("dp", "ctx", None), P(), P("dp", None), P("dp"), P("dp", None), P("dp", "ctx", None), P(), P(),
    )
    return jax.shard_map(
        body,
        mesh=mesh,
        in_specs=placed,
        out_specs=(P("dp", "ctx", None), P("dp", "ctx"), P("dp", "ctx")),
        check_vma=False,
    )
```

```python
import functools
import math

import jax
import jax.numpy as jnp
from jax import lax
from jax.experimental import pallas as pl
from jax.experimental.pallas import tpu as pltpu
from jax.sharding import PartitionSpec as P

MESH = pl.DeviceIdType.MESH
EPS = 1e-06
X, Y, Z, CTX = 4, 4, 8, 32
ROWS, SEG, HID, LLM, VIT = 128, 640, 320, 4096, 2560
HALF = LLM // 2
CHUNKS = tuple((h, pl.ds(r, 32)) for h in range(2) for r in (0, 32))
F32, BF16 = jnp.float32, jnp.bfloat16
NT = (((1,), (1,)), ((), ()))
NN = (((1,), (0,)), ((), ()))
TN = (((0,), (0,)), ((), ()))
dot = functools.partial(lax.dot_general, preferred_element_type=F32)


def place():
    dp, ctx = lax.axis_index("dp"), lax.axis_index("ctx")
    x, y, core = lax.rem(dp, X), ctx // 8, lax.rem(ctx, 2)
    z = lax.rem(ctx // 2, 4) * 2 + dp // X
    return x, y, z, core


def device(x, y, z, core):
    return (lax.rem(z, 2) * X + x, y * 8 + (z // 2) * 2 + core)


def remote(src, dst, send, recv, to):
    return pltpu.make_async_remote_copy(
        src_ref=src, dst_ref=dst, send_sem=send, recv_sem=recv, device_id=to, device_id_type=MESH
    )


def loop(n, body):
    lax.fori_loop(0, n, lambda i, c: (body(i), c)[1], 0)


def part(i, size):
    return pl.ds(pl.multiple_of(i * size, size), size)


def ring_sum(n, me, own, halves, step, bufs, accs, send, recv, to, finish):
    half = n // 2
    copies = []
    for d, sign in enumerate((1, -1)):
        t = lax.rem(me + n + sign * half, n)
        at = pl.ds(*halves[d])
        c = remote(own(t).at[at], bufs.at[d, 0, at], send.at[d, 0], recv.at[d, 0], to[d])
        c.start()
        copies.append(c)
    last = list(copies)
    yield
    for s in range(2, half + 1):
        for d, sign in enumerate((1, -1)):
            t = lax.rem(me + n + sign * (half + 1 - s), n)
            mine, came, out = own(t), bufs.at[d, s - 2], accs.at[d, s - 2]

            def add(first, count, came=came, mine=mine, out=out):
                def one(i):
                    at = pl.ds(pl.multiple_of(first + i * step, step), step)
                    out[at] = (mine[at].astype(F32) + came[at].astype(F32)).astype(BF16)

                loop(count // step, one)

            def carry(first, count, mine=mine, out=out):
                def one(i):
                    at = pl.ds(pl.multiple_of(first + i * step, step), step)
                    out[at] = mine[at]

                loop(count // step, one)

            if s == 2:
                carry(*halves[1 - d])
                last[d].wait_recv()
                add(*halves[d])
            else:
                last[d].wait_recv()
                add(0, out.shape[0])
            c = remote(out, bufs.at[d, s - 1], send.at[d, s - 1], recv.at[d, s - 1], to[d])
            c.start()
            copies.append(c)
            last[d] = c
        yield
    for d in range(2):
        last[d].wait_recv()
    finish(own(me), bufs.at[0, half - 1], bufs.at[1, half - 1])
    for c in copies:
        c.wait_send()


def kernel(
    inv, order, frames, llm, vit, gain, bias, w1, w2,
    out_v, out1, out2,
    masked, recv1a, recv1b, recv1c, recv1d, send2a, send2b, send2c, send2d, n_rows, l_rows, w1v, w2v, bv,
    pre, hg, act, pg, ng,
    act_s, pg_s, t1, t2,
    m1, m2, f1, f2, q1, q2,
    xb, xa, y1b, y1a, z1b, z1a, z2b, z2a, y2b, y2a,
    s1, r1, s2, r2, loc, wsend, wrecv, nsend, nrecv, lsend, lrecv, csend, crecv,
    xs, xr, y1s, y1r, z1s, z1r, z2s, z2r, y2s, y2r, qs, qr,
):
    recv1, send2 = (recv1a, recv1b, recv1c, recv1d), (send2a, send2b, send2c, send2d)
    x, y, z, core = place()
    ctx, dp = lax.axis_index("ctx"), lax.axis_index("dp")
    right, left, far = lax.rem(x + 1, X), lax.rem(x + X - 1, X), lax.rem(x + 2, X)
    up, down = lax.rem(z + 1, Z), lax.rem(z + Z - 1, Z)
    x_to = [device(right, y, z, core), device(left, y, z, core)]
    y_to = [device(x, lax.rem(y + 1, Y), z, core), device(x, lax.rem(y + Y - 1, Y), z, core)]
    z_to = [device(x, y, up, core), device(x, y, down, core)]
    sibling = device(x, y, z, 1 - core)
    z_lo, z_hi = lax.rem(z, 2), z // 2
    swap = device(x, y, z + 1 - 2 * z_lo, 1 - core)

    barrier = pltpu.get_barrier_semaphore()

    def hello(k):
        pl.semaphore_signal(
            barrier, inc=1, device_id=(dp, lax.rem(ctx + k + 1, CTX)), device_id_type=MESH
        )

    loop(CTX - 1, hello)
    for other in x_to + z_to + [swap]:
        pl.semaphore_signal(barrier, inc=1, device_id=other, device_id_type=MESH)

    keep_w = [
        pltpu.make_async_copy(w1, w1v.at[pl.ds(0, HID)], loc.at[0]),
        pltpu.make_async_copy(w2, w2v.at[pl.ds(0, HID)], loc.at[1]),
    ]
    for c in keep_w:
        c.start()

    bv[pl.ds(0, HID)] = jnp.broadcast_to(bias[...][None, :], (128, HID)).T

    def norm(i):
        rows = part(i, 32)
        for seg in range(4):
            cols = slice(seg * SEG, (seg + 1) * SEG)
            states = vit[rows, cols].astype(F32)
            inv_rms = lax.rsqrt(jnp.mean(states * states, axis=-1, keepdims=True) + EPS)
            n_rows[0, x, i // 2, part(lax.rem(i, 2), 32), cols] = (
                states * inv_rms * gain[...][None, :]
            ).astype(BF16)

    loop(4, norm)

    t0 = order[2 * ctx]
    t1_ = order[2 * ctx + 1]
    low_first = lax.rem(t0 // 4, 4) < 2
    for b in range(2):
        at_first = low_first if b == 0 else jnp.logical_not(low_first)
        index = jnp.where(at_first, 0, 1)
        t = jnp.where(at_first, t0, t1_)
        for frame in range(2):
            count = frames[dp, 2 * t + frame]
            keep = lax.broadcasted_iota(jnp.int32, (32, 512), 0) < count
            rows = pl.ds(32 * frame, 32)

            def mask(c, b=b, index=index, keep=keep, rows=rows):
                cols = part(c, 512)
                masked[b, rows, cols] = jnp.where(
                    keep, llm[index, rows, cols].astype(F32), 0.0
                ).astype(BF16)

            loop(8, mask)

    pl.semaphore_wait(barrier, CTX - 1 + 5)

    def spread(piece, send, recv):
        own = piece(x, slice(0, 2))
        return [remote(own, own, send.at[d], recv.at[d], x_to[d]) for d in range(2)]

    def forward(piece, send, recv):
        out = []
        for d, slot in enumerate((left, right)):
            one = piece(slot, d)
            out.append(remote(one, one, send.at[2 + d], recv.at[2 + d], x_to[d]))
        return out

    def start(copies):
        for c in copies:
            c.start()

    def received(copies):
        for c in copies:
            c.wait_recv()

    def n_piece(slot, block):
        return n_rows.at[0, slot, block]

    n_a = spread(n_piece, nsend, nrecv)
    n_f = forward(n_piece, nsend, nrecv)

    def q_of(m):
        return (m // 8) * 4 + lax.rem(m, 4)

    def b_of(m):
        return lax.rem(m // 4, 2)

    q = q_of(ctx)

    def strip(h, k):
        return pl.ds(pl.multiple_of(h * HALF + k * 128, 128), 128)

    def first(c, k):
        h, rows = CHUNKS[c]
        m = lax.rem(ctx + k + 1, CTX)
        return remote(
            masked.at[b_of(m), rows, strip(h, q_of(m))], recv1[c].at[ctx], s1.at[c, k], r1.at[c, ctx], (dp, m)
        )

    def first_here(c, k):
        h, rows = CHUNKS[c]
        s = lax.rem(ctx + k + 1, CTX)
        return remote(masked.at[0, rows, strip(h, 0)], recv1[c].at[s], s1.at[c, k], r1.at[c, s], (dp, s))

    own1 = [
        pltpu.make_async_copy(masked.at[b_of(ctx), rows, strip(h, q)], recv1[c].at[ctx], loc.at[2 + c])
        for c, (h, rows) in enumerate(CHUNKS)
    ]

    def offer(c):
        loop(CTX - 1, lambda k: first(c, k).start())
        own1[c].start()

    def owner(e):
        return (e // 4) * 8 + b_of(ctx) * 4 + lax.rem(e, 4)

    def pick(c, e):
        for i in range(2):
            block = inv[2 * owner(e) + i]
            send2[c][e, i] = recv1[c][block // 2]

    def landing(c, k):
        h, rows = CHUNKS[c]
        return l_rows.at[0, x, :, rows, strip(h, k)]

    def second(c, k):
        e = lax.rem(q + k + 1, 16)
        return remote(send2[c].at[e], landing(c, q), s2.at[c, k], r2.at[c, q], (dp, owner(e)))

    def second_here(c, k):
        e = lax.rem(q + k + 1, 16)
        return remote(send2[c].at[e], landing(c, e), s2.at[c, k], r2.at[c, e], (dp, owner(e)))

    own2 = [
        pltpu.make_async_copy(send2[c].at[q], landing(c, q), loc.at[6 + c])
        for c in range(len(CHUNKS))
    ]

    def reorder(c):
        loop(CTX - 1, lambda k: first_here(c, k).wait_recv())
        own1[c].wait()

        def send(k):
            pick(c, lax.rem(q + k + 1, 16))
            second(c, k).start()

        loop(15, send)
        pick(c, q)
        own2[c].start()

    def reordered(c):
        loop(15, lambda k: second_here(c, k).wait_recv())
        own2[c].wait()

    to_z = device(x, y, jnp.where(core == 0, up, down), core)
    y_next, y_prev, y_far = lax.rem(y + 1, Y), lax.rem(y + Y - 1, Y), lax.rem(y + 2, Y)
    w_cols = [pl.ds(pl.multiple_of(core * (n // 2), 128), n // 2) for n in (VIT, LLM)]
    w_in, w_at = (w1, w2), (w1v, w2v)

    def quarter(r, yy, first_row, count):
        return w_at[r].at[pl.ds(pl.multiple_of(HID + yy * 80 + first_row, 16), count), w_cols[r]]

    w_z, w_y, w_f, w_c = [], [[], []], [[], []], []
    for r in range(2):
        own_quarter = w_in[r].at[pl.ds(pl.multiple_of(y * 80, 16), 80), w_cols[r]]
        here = quarter(r, y, 0, 80)
        w_z.append(remote(own_quarter, here, wsend.at[r, 0], wrecv.at[r, 0], to_z))
        for d, (slot, at) in enumerate(((y_prev, (0, 48)), (y_next, (48, 32)))):
            w_y[r].append(remote(here, here, wsend.at[r, 1 + d], wrecv.at[r, 1 + d], y_to[d]))
            piece = quarter(r, slot, *at)
            w_f[r].append(remote(piece, piece, wsend.at[r, 3 + d], wrecv.at[r, 3 + d], y_to[d]))
        share = w_at[r].at[pl.ds(HID, HID), w_cols[r]]
        w_c.append(remote(share, share, wsend.at[r, 5], wrecv.at[r, 5], sibling))
    w_z.append(remote(bv.at[pl.ds(0, HID)], bv.at[pl.ds(HID, HID)], wsend.at[2, 0], wrecv.at[2, 0], to_z))

    def weights_round(r):
        w_z[r].wait_recv()
        start(w_y[r])

    def weights_on(r):
        received(w_y[r])
        start(w_f[r])

    def weights_share(r):
        received(w_f[r])
        w_c[r].start()

    def group(k):
        return pl.ds(k * HID, HID)

    def activate(k):
        pre[group(k)] = dot(w1v[group(k)], n_rows[0].reshape(X * ROWS, VIT), NT)

        def chunk(i):
            at = pl.ds(pl.multiple_of(k * HID + i * 32, 32), 32)
            v = pre[at] + bv[at, :1]
            cdf = 0.5 * (1.0 + lax.erf(v * (1.0 / math.sqrt(2.0))))
            density = jnp.exp(-0.5 * v * v) * (1.0 / math.sqrt(2.0 * math.pi))
            act[at] = (v * cdf).astype(BF16)
            pre[at] = cdf + v * density

        loop(10, chunk)

    def tokens(slot):
        return part(slot, ROWS)

    def hidden(slot, h, k):
        cols = pl.ds(h * HALF, HALF)
        got = dot(w2v[group(k), cols], l_rows[0, slot, :, :, cols].reshape(ROWS, HALF), NT)
        if h == 0:
            hg[group(k), tokens(slot)] = got
        else:
            hg[group(k), tokens(slot)] += got

    def pre_grad(slot):
        def chunk(i):
            at = part(i, 64)
            pg[at, tokens(slot)] = (hg[at, tokens(slot)] * pre[at, tokens(slot)]).astype(BF16)

        loop(10, chunk)

    def gradient(slot):
        for c in range(2):
            cols = slice(c * 1280, (c + 1) * 1280)
            ng[slot, :, cols] = dot(pg[:, tokens(slot)], w1v[:, cols], TN).astype(BF16)

    mine = lax.rem(z_lo + core, 2)
    own_h, other_h = (pl.ds(pl.multiple_of(k * HID, HID), HID) for k in (mine, 1 - mine))

    def share(src, dst, i):
        return remote(src, dst, csend.at[i], crecv.at[i], sibling)

    def share_l(h, rows, slots, i):
        cols = l_cols[h]
        return share(l_rows.at[0, slots, :, rows, cols], l_rows.at[1, slots, :, rows, cols], i)

    l_cols = [pl.ds(h * HALF, HALF) for h in range(2)]
    c_n = share(n_rows.at[0], n_rows.at[1], 0)
    c_act = share(act.at[other_h], act_s, 1)
    slots = (x, left, right, far)
    c_pg = [share(pg.at[other_h, tokens(slot)], pg_s.at[:, tokens(slot)], 9 + i) for i, slot in enumerate(slots)]
    c_l = [share_l(0, slice(0, 64), slice(0, X), 3), share_l(1, slice(0, 32), slice(0, X), 4)]
    c_last = [share_l(1, slice(32, 64), slot, 5 + i) for i, slot in enumerate(slots)]

    def second_grad(h, c):
        cols = slice(h * HALF + c * 512, h * HALF + (c + 1) * 512)
        rows = [l_rows[k, :, :, :, cols].reshape(X * ROWS, 512) for k in range(2)]
        got = (dot(act[own_h], rows[0], NN) + dot(act_s[...], rows[1], NN)).astype(BF16)
        for i in range(4):
            t2[h, (4 * c + i) % Z, c // 2] = got[:, i * 128 : (i + 1) * 128]

    def first_grad(yy):
        cols = part(yy, SEG)
        rows = [n_rows[k, :, :, :, cols].reshape(X * ROWS, SEG) for k in range(2)]
        t1[yy] = (dot(pg[own_h], rows[0], NN) + dot(pg_s[...], rows[1], NN)).astype(BF16)

    def keep2(h):
        def finish(own, a, b):
            for i in range(2):
                m2[2 * h + i] = (
                    own[i].astype(F32) + a[i].astype(F32) + b[i].astype(F32)
                ).astype(BF16)

        return finish

    def keep1(own, a, b):
        for c in range(5):
            cols = slice(c * 128, (c + 1) * 128)
            total = own[:, cols].astype(F32) + a[:, cols].astype(F32) + b[:, cols].astype(F32)
            m1[cols] = total.T.astype(BF16)

    def last(f):
        def finish(own, a, b):
            f[...] = own[...].astype(F32) + a[...].astype(F32) + b[...].astype(F32)

        return finish

    def finish_x(own, a, b):
        def rows(i):
            at = part(i, 16)
            for seg in range(4):
                cols = slice(seg * SEG, (seg + 1) * SEG)
                grad = (
                    own[at, cols].astype(F32) + a[at, cols].astype(F32) + b[at, cols].astype(F32)
                )
                states = vit[at, cols].astype(F32)
                inv_rms = lax.rsqrt(jnp.mean(states * states, axis=-1, keepdims=True) + EPS)
                scaled = states * inv_rms
                g = grad * gain[...][None, :]
                out_v[at, cols] = (
                    inv_rms * (g - scaled * jnp.mean(g * scaled, axis=-1, keepdims=True))
                ).astype(BF16)

        loop(8, rows)

    x_ring = ring_sum(
        X, x, lambda t: ng.at[t], ((0, 64), (64, 64)), 16, xb, xa, xs, xr, x_to, finish_x
    )
    z2_rings = [
        ring_sum(
            Z, z, lambda t, h=h: t2.at[h, t], ((0, 1), (1, 1)), 1,
            z2b.at[h], z2a.at[h], z2s.at[h], z2r.at[h], z_to, keep2(h),
        )
        for h in range(2)
    ]
    y2_ring = ring_sum(
        Y, y, lambda t: m2.at[t], ((0, 160), (160, 160)), 160, y2b, y2a, y2s, y2r, y_to, last(f2)
    )
    y1_ring = ring_sum(
        Y, y, lambda t: t1.at[t], ((0, 160), (160, 160)), 32, y1b, y1a, y1s, y1r, y_to, keep1
    )
    z1_ring = ring_sum(
        Z, z, lambda t: m1.at[part(t, 80)], ((0, 48), (48, 32)), 16, z1b, z1a, z1s, z1r, z_to, last(f1)
    )

    def run(*rings):
        for r in rings:
            next(r, None)

    def l_piece(c):
        h, rows = CHUNKS[c]
        return lambda slot, block: l_rows.at[0, slot, block, rows, l_cols[h]]

    l_a = [spread(l_piece(c), lsend.at[c], lrecv.at[c]) for c in range(4)]
    l_f = [forward(l_piece(c), lsend.at[c], lrecv.at[c]) for c in range(4)]

    start(n_a)
    offer(0)
    offer(1)
    reorder(0)
    start(w_z)
    offer(2)
    received(n_a)
    start(n_f)
    reordered(0)
    start(l_a[0])
    reorder(1)
    offer(3)
    weights_round(0)
    weights_round(1)
    received(n_f)
    c_n.start()
    reordered(1)
    start(l_a[1])
    received(l_a[0])
    start(l_f[0])
    reorder(2)
    weights_on(0)
    weights_on(1)
    for c in keep_w:
        c.wait()
    activate(0)
    received(l_a[1])
    start(l_f[1])
    weights_share(0)
    weights_share(1)
    reordered(2)
    start(l_a[2])
    reorder(3)
    w_c[0].wait_recv()
    w_z[2].wait_recv()
    activate(1)
    c_act.start()
    received(l_a[2])
    start(l_f[2])
    received(l_f[0])
    received(l_f[1])
    c_l[0].start()
    w_c[1].wait_recv()
    for slot in (x, left):
        for k in range(2):
            hidden(slot, 0, k)
    reordered(3)
    start(l_a[3])
    for slot in (right, far):
        for k in range(2):
            hidden(slot, 0, k)
    c_act.wait_recv()
    c_l[0].wait_recv()
    c_n.wait_recv()
    second_grad(0, 0)
    second_grad(0, 1)
    received(l_a[3])
    start(l_f[3])
    start(c_last[:3])
    second_grad(0, 2)
    second_grad(0, 3)
    run(z2_rings[0])
    received(l_f[2])
    c_l[1].start()
    for i in range(3):
        for k in range(2):
            hidden(slots[i], 1, k)
        pre_grad(slots[i])
        c_pg[i].start()
    received(l_f[3])
    c_last[3].start()
    for k in range(2):
        hidden(far, 1, k)
    pre_grad(far)
    c_pg[3].start()
    gradient(far)
    run(x_ring)
    run(z2_rings[0])
    received(c_pg)
    first_grad(y_far)
    run(y1_ring)
    run(z2_rings[0])
    c_l[1].wait_recv()
    received(c_last)
    for c in range(4):
        second_grad(1, c)
    run(z2_rings[1])
    first_grad(y_next)
    first_grad(y_prev)
    run(y1_ring)
    run(z2_rings[0])
    gradient(left)
    gradient(right)
    run(x_ring)
    run(z2_rings[1])
    run(z2_rings[0])
    run(z2_rings[1])
    first_grad(y)
    gradient(x)
    run(z2_rings[1])
    run(y1_ring)
    run(z1_ring)
    run(z2_rings[1])
    run(y2_ring)
    run(z1_ring)
    run(z1_ring)
    run(y2_ring)
    run(z1_ring)
    run(y2_ring)

    away = core != z_lo
    home = [remote(q.at[0], q.at[1], qs.at[i], qr.at[i], swap) for i, q in enumerate((q1, q2))]

    @pl.when(away)
    def _():
        q2[0] = f2[...].astype(BF16)
        home[1].start()

    run(z1_ring)

    @pl.when(away)
    def _():
        q1[0] = f1[...].astype(BF16)
        home[0].start()

    run(x_ring)

    @pl.when(away)
    def _():
        home[1].wait()
        out2[...] = q2[1].astype(F32)
        home[0].wait()
        out1[...] = q1[1].astype(F32)

    @pl.when(jnp.logical_not(away))
    def _():
        out1[...] = f1[...]
        out2[...] = f2[...]

    for c in n_a + n_f + sum(l_a + l_f + w_y + w_f, []) + w_z + w_c + c_l + c_last + c_pg + [c_n, c_act]:
        c.wait_send()
    for i in range(4):
        loop(CTX - 1, lambda k, i=i: first(i, k).wait_send())
        loop(15, lambda k, i=i: second(i, k).wait_send())


def fused(inv, order, frames, llm, vit, gain, bias, w1, w2):
    any_, vmem, smem = (pl.BlockSpec(memory_space=m) for m in (pl.ANY, pltpu.VMEM, pltpu.SMEM))
    dma = pltpu.SemaphoreType.DMA

    def v(*shape, dtype=BF16):
        return pltpu.VMEM(shape, dtype)

    f32 = functools.partial(v, dtype=F32)
    pairs = [(4, CTX), (4, 16)]
    sems = []
    for shape in pairs:
        sems += [dma(shape), dma(shape)]
    sems += [dma((10,))]
    for shape in ((3, 6), (4,), (4, 4), (13,), (2, 2), (2, 2), (2, 4), (2, 2, 4), (2, 2), (2,)):
        sems += [dma(shape), dma(shape)]
    return pl.pallas_call(
        kernel,
        out_shape=(
            jax.ShapeDtypeStruct((ROWS, VIT), BF16),
            jax.ShapeDtypeStruct((80, HID), F32),
            jax.ShapeDtypeStruct((HID, 128), F32),
        ),
        in_specs=[smem, smem, smem, vmem, vmem, vmem, vmem, any_, any_],
        out_specs=[vmem] * 3,
        scratch_shapes=[
            v(2, 64, LLM), *[v(CTX, 32, 128)] * 4, *[v(16, 2, 32, 128)] * 4,
            v(2, X, 2, 64, VIT), v(2, X, 2, 64, LLM),
            v(2 * HID, VIT), v(2 * HID, LLM), f32(2 * HID, 128),
            f32(2 * HID, X * ROWS), f32(2 * HID, X * ROWS),
            v(2 * HID, X * ROWS), v(2 * HID, X * ROWS), v(X, ROWS, VIT),
            v(HID, X * ROWS), v(HID, X * ROWS),
            v(Y, HID, SEG), v(2, Z, 2, HID, 128),
            v(SEG, HID), v(Y, HID, 128), f32(80, HID), f32(HID, 128),
            v(2, 80, HID), v(2, HID, 128),
            v(2, 2, ROWS, VIT), v(2, 1, ROWS, VIT),
            v(2, 2, HID, SEG), v(2, 1, HID, SEG),
            v(2, 4, 80, HID), v(2, 3, 80, HID),
            v(2, 2, 4, 2, HID, 128), v(2, 2, 3, 2, HID, 128),
            v(2, 2, HID, 128), v(2, 1, HID, 128),
        ] + sems,
        compiler_params=pltpu.CompilerParams(
            collective_id=0, has_side_effects=True, vmem_limit_bytes=60 * 2**20
        ),
        name="fused",
    )(inv, order, frames, llm, vit, gain, bias, w1, w2)


def body(vit_states, norm_gain, w_first, b_first, w_second, llm_grad, block_order, frame_tokens):
    positions = jnp.arange(64, dtype=jnp.int32)
    matches = (block_order[None, :] == positions[:, None]).astype(jnp.int32)
    inverse = jnp.sum(matches * positions[None, :], axis=1)
    vit_grad, first, second = fused(
        inverse, block_order, frame_tokens, llm_grad.reshape(2, 64, LLM), vit_states[0],
        norm_gain, b_first, w_first, w_second,
    )
    return (vit_grad[None], first.T, second)


def solution(mesh):
    placed = (
        P("dp", "ctx", None), P(), P("dp", None), P("dp"), P("dp", None), P("dp", "ctx", None), P(), P(),
    )
    return jax.shard_map(
        body,
        mesh=mesh,
        in_specs=placed,
        out_specs=(P("dp", "ctx", None), P("dp", "ctx"), P("dp", "ctx")),
        check_vma=False,
    )
```
